32 devices in a mesh: order: 8 (over z, x), blk: 4 (over y, core).
Axes of the slice: x: 2, y: 2, z: 4, core: 2. Of those that a mesh axis runs over, the one named last changes fastest.
Arguments:
- fourier_cycles: float32 [16, 128, 128], P('order', 'blk'), parts along dimension 0, may hold values from -6 to 6
- legendre: float32 [16, 128, 12288], P('order', 'blk'), parts along dimension 0, may hold values from -0.5 to 0.5
- cycle_weight: float32 [128], P('blk'), may hold values from 0.5 to 2
- matched_filter_weights: float32 [12288, 8, 8], P('blk'), may hold values from -2 to 2
- cluster_cycles: int32 [16, 64], P('order'), parts along dimension 0, may hold values from 0 to 127
- cluster_flux: float32 [16, 64, 128], P('order'), parts along dimension 0, may hold values from -18 to 18
- order_per_slot: int32 [16], P('order'), parts along dimension 0, may hold values from 0 to 6143
Outputs:
- synthesized: float32 [16, 128, 128], P('order', 'blk'), parts along dimension 0
The draws below stay inside these ranges and needn't reach their ends.
There are 8 independent parts, one for each index of `order`. The reference program is written for one: setup_inputs(seed, part) draws one part's arguments, and reference() takes and returns one part's arrays. A program takes and returns all parts, laid end to end along the dimension named above; an argument that names none is the same for every part. Nothing has to cross between parts.
Inputs may be any that keep to these rules, and one draw needn't show every extreme that they name: `cluster_cycles`: cycle indices; several clusters may share a cycle, and their coefficients add. `order_per_slot`: order of each slot; degrees below it carry no coefficients.
All inputs are finite; a program needn't handle non-finite values.
Results may differ from the reference program's by a relative error of at most 0.00011.
Values sent between devices are 32-bit elements; how exact they have to be, the bound alone decides.
No kernel may reach another device: no remote copies, remote signals or barrier semaphores. Data moves between devices by JAX's collectives and lax.ppermute only.
A program may use at most 192 MiB of HBM per device.

```python
import math
import jax
import jax.numpy as jnp
from jax import lax

L = 12288
F = 8
S = 8
SIMS = 8
M = 2
CLUSTERS = 64
R = 128


def with_ends(array, own_key, low, high):
    dims = array.shape
    index_at = [jax.random.randint(jax.random.fold_in(own_key, axis), (), 0, dims[axis]) for axis in range(len(dims))]
    array = array.at[tuple(index_at)].set(low)
    longest = dims.index(max(dims))
    index_at[longest] = (index_at[longest] + 1) % dims[longest]
    return array.at[tuple(index_at)].set(high)


def level_of(own_key, shape, shards, low, top_value):
    gain = 1.0
    for position, shards_of in shards:
        draws = jax.random.uniform(jax.random.fold_in(jax.random.fold_in(own_key, 6), position), (shards_of,), jnp.float32, low / len(shards), top_value / len(shards))
        gain = gain * jnp.repeat(jnp.exp(draws), shape[position] // shards_of).reshape((-1,) + (1,) * (len(shape) - 1 - position))
    return gain


def normal_values(rng, extent, deviation, bound, split=(), kind=jnp.bfloat16):
    array = jax.random.normal(rng, extent, jnp.float32) * deviation
    if len(split) > 0:
        array = level_of(rng, extent, split, -0.22, 0.18) * array
    return jnp.clip(array, min=-bound, max=bound).astype(kind)


def setup_inputs(seed: int = 0, part: int = 0) -> dict:
    arg_keys = jax.random.split(jax.random.key(seed), 8)
    part_keys = jax.random.split(jax.random.fold_in(arg_keys[7], part), 8)
    fourier_cycles = normal_values(part_keys[0], (M, R, 2 * F * SIMS), 1.0, 6.0, ((1, 4),), jnp.float32)
    legendre = normal_values(part_keys[1], (M, R, L), R ** -0.5, 0.5, ((1, 4),), jnp.float32)
    cycle_weight = jnp.clip(jnp.exp(math.log(2.0) - 1.3862944 * jax.random.uniform(arg_keys[2], (R,), jnp.float32) ** level_of(arg_keys[2], (R,), ((0, 4),), -0.2, 0.2)), 0.5, 2.0)
    matched_filter_weights = normal_values(arg_keys[3], (L, S, F), F ** -0.5, 2.0, ((0, 4),), jnp.float32)
    cluster_cycles = with_ends(jax.random.randint(part_keys[4], (M, CLUSTERS), 0, R), jax.random.fold_in(part_keys[4], 1), 0, R - 1).astype(jnp.int32)
    cluster_flux = normal_values(part_keys[5], (M, CLUSTERS, 2 * F * SIMS), 3.0, 18.0, (), jnp.float32)
    order_per_slot = jax.random.randint(part_keys[6], (M,), 0, L // 2).astype(jnp.int32)
    return {"fourier_cycles": fourier_cycles, "legendre": legendre, "cycle_weight": cycle_weight, "matched_filter_weights": matched_filter_weights, "cluster_cycles": cluster_cycles, "cluster_flux": cluster_flux, "order_per_slot": order_per_slot}


highest_degree = lax.Precision.HIGHEST

def inject(fourier_cycles, cycle_weight, cluster_cycles, cluster_flux, cycle_ids):
    cycle_hits = (cycle_ids[None, :, None] == cluster_cycles[:, None, :]).astype(jnp.float32)
    added = jnp.einsum('krj,kjc->krc', cycle_hits, cluster_flux, precision=highest_degree)
    return cycle_weight[None, :, None] * (fourier_cycles + added)

def apply_filter(harmonics, matched_filter_weights, degrees, order_per_slot):
    kept_mask = (degrees[:, None] >= order_per_slot[None, :]).astype(jnp.float32)
    blocks = harmonics.shape[0]
    masked_values = (harmonics * kept_mask[:, :, None]).reshape(blocks, M, 2, F, SIMS)
    matched_output = jnp.einsum('dvr,dotrq->dotvq', matched_filter_weights, masked_values, precision=highest_degree)
    squares = lax.optimization_barrier(jnp.sum(matched_filter_weights * matched_filter_weights, axis=2))
    weights = kept_mask * (2.0 * degrees.astype(jnp.float32) + 1.0)[:, None]
    response = jnp.einsum('lk,ls->ks', weights, squares, precision=highest_degree)
    return (matched_output, response)

def reference(fourier_cycles, legendre, cycle_weight, matched_filter_weights, cluster_cycles, cluster_flux, order_per_slot):
    cycle_ids = jnp.arange(fourier_cycles.shape[1], dtype=jnp.int32)
    injected = inject(fourier_cycles, cycle_weight, cluster_cycles, cluster_flux, cycle_ids)
    harmonics = jnp.einsum('krl,krc->lkc', legendre, injected, precision=highest_degree)
    degrees = jnp.arange(L, dtype=jnp.int32)
    matched_output, response = apply_filter(harmonics, matched_filter_weights, degrees, order_per_slot)
    scaled = matched_output * (L / jnp.sqrt(response))[None, :, None, :, None]
    scaled = scaled.reshape(L, M, 2 * S * SIMS)
    return jnp.einsum('krl,lkc->krc', legendre, scaled, precision=highest_degree)
```

```python
import functools

import jax
import jax.numpy as jnp
from jax import lax
from jax.experimental import pallas as pl
from jax.experimental.pallas import tpu as pltpu
from jax.sharding import PartitionSpec as P

LANES = 128
VMEM_LIMIT = 48 * 1024 * 1024


def partner(x, n):
    return [(i, i ^ x) for i in range(n)]


def split_degrees(blocks):
    tiles = blocks // LANES
    if tiles < 12:
        return [blocks]
    first = tiles // 6
    last = tiles // 12
    middle = tiles - first - last
    half = middle // 2
    return [w * LANES for w in (first, half, middle - half, last)]


def halves(value):
    high = value.astype(jnp.bfloat16)
    low = (value - high.astype(jnp.float32)).astype(jnp.bfloat16)
    return high, low


def compiler_params(**kwargs):
    return pltpu.CompilerParams(vmem_limit_bytes=VMEM_LIMIT, **kwargs)


def cut_kernel(pieces, blocks, me_ref, legendre_ref, *refs):
    outs, sems = refs[:-1], refs[-1]
    copies = []
    for number, (x, offset, width) in enumerate(pieces):
        start = pl.multiple_of((me_ref[0] ^ x) * blocks + offset, LANES)
        copies.append(
            pltpu.make_async_copy(
                legendre_ref.at[:, :, pl.ds(start, width)], outs[number], sems.at[number]
            )
        )
    for copy in copies:
        copy.start()
    for copy in copies:
        copy.wait()


def cut(me, legendre, pieces, blocks):
    orders, rows, _ = legendre.shape
    shapes = [jax.ShapeDtypeStruct((orders, rows, w), jnp.float32) for _, _, w in pieces]
    size = sum(orders * rows * w * 4 for _, _, w in pieces)
    return pl.pallas_call(
        functools.partial(cut_kernel, pieces, blocks),
        out_shape=shapes,
        in_specs=[pl.BlockSpec(memory_space=pltpu.SMEM), pl.BlockSpec(memory_space=pl.ANY)],
        out_specs=[pl.BlockSpec(memory_space=pl.ANY)] * len(pieces),
        scratch_shapes=[pltpu.SemaphoreType.DMA((len(pieces),))],
        compiler_params=compiler_params(),
        cost_estimate=pl.CostEstimate(flops=0, bytes_accessed=2 * size, transcendentals=0),
        name="cut",
    )(me, legendre)


def inject_kernel(me_ref, cycles_ref, weight_ref, hits_ref, flux_ref, out_ref):
    orders, rows, _ = cycles_ref.shape
    count = hits_ref.shape[1]
    eye = lax.broadcasted_iota(jnp.int32, (rows, rows), 0) == lax.broadcasted_iota(
        jnp.int32, (rows, rows), 1
    )
    weight = jnp.sum(jnp.where(eye, weight_ref[...], 0.0), axis=1, keepdims=True)
    ids = me_ref[0] * rows + lax.broadcasted_iota(jnp.int32, (rows, count), 0)
    for k in range(orders):
        hits = (ids == hits_ref[k : k + 1, :]).astype(jnp.float32)
        added = jnp.dot(
            hits,
            flux_ref[k],
            precision=lax.Precision.HIGHEST,
            preferred_element_type=jnp.float32,
        )
        out_ref[k] = weight * (cycles_ref[k] + added)


def inject(me, cycles, weight, cluster_cycles, flux):
    vmem = pl.BlockSpec(memory_space=pltpu.VMEM)
    return pl.pallas_call(
        inject_kernel,
        out_shape=jax.ShapeDtypeStruct(cycles.shape, jnp.float32),
        in_specs=[pl.BlockSpec(memory_space=pltpu.SMEM), vmem, vmem, vmem, vmem],
        out_specs=vmem,
        compiler_params=compiler_params(),
        name="inject",
    )(me, cycles, weight.reshape(1, -1), cluster_cycles, flux)


def response_kernel(blocks, scales, skies, me_ref, order_ref, weights_ref, out_ref):
    orders = order_ref.shape[0]
    degree = me_ref[0] * blocks + lax.broadcasted_iota(jnp.int32, (1, blocks), 1)
    factor = 2.0 * degree.astype(jnp.float32) + 1.0
    squares = jnp.concatenate(
        [
            jnp.sum(weights_ref[s] * weights_ref[s], axis=0, keepdims=True) * factor
            for s in range(scales)
        ],
        axis=0,
    )
    columns = out_ref.shape[1]
    scale_of = (lax.broadcasted_iota(jnp.int32, (scales, columns), 1) // skies) % scales
    chosen = scale_of == lax.broadcasted_iota(jnp.int32, (scales, columns), 0)
    out_ref[...] = jnp.zeros_like(out_ref)
    for k in range(orders):
        total = jnp.sum(jnp.where(degree >= order_ref[k], squares, 0.0), axis=1, keepdims=True)
        out_ref[k : k + 1, :] = jnp.sum(jnp.where(chosen, total, 0.0), axis=0, keepdims=True)


def response_rows(me, order_per_slot, weights, skies, columns):
    scales, _, blocks = weights.shape
    smem = pl.BlockSpec(memory_space=pltpu.SMEM)
    vmem = pl.BlockSpec(memory_space=pltpu.VMEM)
    rows = -(-order_per_slot.shape[0] // 8) * 8
    return pl.pallas_call(
        functools.partial(response_kernel, blocks, scales, skies),
        out_shape=jax.ShapeDtypeStruct((rows, columns), jnp.float32),
        in_specs=[smem, smem, vmem],
        out_specs=vmem,
        compiler_params=compiler_params(),
        name="response",
    )(me, order_per_slot, weights)


def prepare_kernel(*refs):
    pieces, out_ref = refs[:-1], refs[-1]
    for k in range(out_ref.shape[0]):
        whole = jnp.concatenate([piece[k] for piece in pieces], axis=0).T
        high, low = halves(whole)
        out_ref[k] = jnp.concatenate([high, low, high], axis=1)


def prepare(pieces):
    orders, rows, columns = pieces[0].shape
    vmem = pl.BlockSpec(memory_space=pltpu.VMEM)
    return pl.pallas_call(
        prepare_kernel,
        out_shape=jax.ShapeDtypeStruct((orders, columns, 3 * rows * len(pieces)), jnp.bfloat16),
        in_specs=[vmem] * len(pieces),
        out_specs=vmem,
        compiler_params=compiler_params(),
        name="prepare",
    )(*pieces)


def chunk_kernel(n, first, last, blocks, offset, tile, me_ref, order_ref, *refs):
    legendre = refs[:n]
    analysis_ref, weights_ref = refs[n : n + 2]
    rest = list(refs[n + 2 :])
    before = None if first else rest.pop(0)
    response = rest.pop(0) if last else None
    total = rest.pop()
    step = pl.program_id(0)
    orders, rows, _ = legendre[0].shape
    scales, channels, _ = weights_ref.shape
    columns = analysis_ref.shape[1]
    skies = columns // (2 * channels)
    everything = n * rows

    @pl.when(step == 0)
    def _():
        total[...] = jnp.zeros_like(total)

    degree = (
        me_ref[0] * blocks
        + offset
        + step * tile
        + lax.broadcasted_iota(jnp.int32, (1, tile), 1)
    )
    for k in range(orders):
        values = jnp.concatenate([block[k] for block in legendre], axis=0)
        high, low = halves(values)
        harmonics = jnp.dot(
            analysis_ref[k],
            jnp.concatenate([high, high, low], axis=0),
            preferred_element_type=jnp.float32,
        )
        harmonics = jnp.where(degree >= order_ref[k], harmonics, 0.0)
        matched = []
        for p in range(2):
            for s in range(scales):
                value = None
                for f in range(channels):
                    at = (p * channels + f) * skies
                    term = weights_ref[s, f : f + 1, :] * harmonics[at : at + skies, :]
                    value = term if value is None else value + term
                matched.append(value)
        matched_high, matched_low = halves(jnp.concatenate(matched, axis=0))
        total[k] += lax.dot_general(
            jnp.concatenate([high, low], axis=0),
            jnp.concatenate([matched_high, matched_low], axis=0),
            (((1,), (1,)), ((), ())),
            preferred_element_type=jnp.float32,
        )

    @pl.when(step == pl.num_programs(0) - 1)
    def _():
        wide = total.shape[2] // 2
        for k in range(orders):
            result = (
                (total[k, everything:, wide:] + total[k, everything:, :wide])
                + total[k, :everything, wide:]
            ) + total[k, :everything, :wide]
            if before is not None:
                result = result + before[k]
            if last:
                for x in range(n):
                    rest[x][k * rows : (k + 1) * rows, :] = result[x * rows : (x + 1) * rows, :]
            else:
                rest[0][k] = result
        if last:
            for x in range(n):
                rest[x][orders * rows :, :] = response[...]


def chunk(me, order_per_slot, legendre, parts, analysis, weights, before, response, blocks, offset, width):
    n = len(parts) + 1
    orders, rows, _ = legendre.shape
    columns = analysis.shape[1]
    scales, channels, _ = weights.shape
    tile = next(t for t in (512, 384, 256, 128) if width % t == 0 and offset % t == 0 and blocks % t == 0)
    last = response is not None
    first = before is None
    steps = width // tile

    def at(start):
        return pl.BlockSpec((orders, rows, tile), lambda i, me, order: (0, 0, start // tile + i))

    own = pl.BlockSpec(
        (orders, rows, tile),
        lambda i, me, order: (0, 0, me[0] * (blocks // tile) + offset // tile + i),
    )
    whole = lambda array: pl.BlockSpec(array.shape, lambda i, me, order: (0,) * array.ndim)
    operands = [legendre] + [array for array, _ in parts] + [analysis, weights]
    in_specs = [own] + [at(start) for _, start in parts]
    in_specs += [
        whole(analysis),
        pl.BlockSpec((scales, channels, tile), lambda i, me, order: (0, 0, offset // tile + i)),
    ]
    if not first:
        operands.append(before)
        in_specs.append(whole(before))
    if last:
        operands.append(response)
        in_specs.append(whole(response))
        out_shape = [
            jax.ShapeDtypeStruct((orders * rows + response.shape[0], columns), jnp.float32)
        ] * n
    else:
        out_shape = [jax.ShapeDtypeStruct((orders, n * rows, columns), jnp.float32)]
    macs = orders * width * columns * rows * n
    return pl.pallas_call(
        functools.partial(chunk_kernel, n, first, last, blocks, offset, tile),
        out_shape=out_shape,
        grid_spec=pltpu.PrefetchScalarGridSpec(
            num_scalar_prefetch=2,
            grid=(steps,),
            in_specs=in_specs,
            out_specs=[whole(shape) for shape in out_shape],
            scratch_shapes=[pltpu.VMEM((orders, 2 * n * rows, 2 * columns), jnp.float32)],
        ),
        compiler_params=compiler_params(dimension_semantics=("arbitrary",)),
        cost_estimate=pl.CostEstimate(
            flops=2 * 7 * macs,
            bytes_accessed=4 * orders * n * rows * width,
            transcendentals=0,
        ),
        name="chunk",
    )(me, order_per_slot, *operands)


def finish_kernel(degrees, *refs):
    parts, out_ref = refs[:-1], refs[-1]
    orders, rows, _ = out_ref.shape
    total = parts[0][...]
    for part in parts[1:]:
        total = total + part[...]
    for k in range(orders):
        at = orders * rows + k
        out_ref[k] = total[k * rows : (k + 1) * rows, :] * (
            degrees / jnp.sqrt(total[at : at + 1, :])
        )


def finish(parts, shape, degrees):
    vmem = pl.BlockSpec(memory_space=pltpu.VMEM)
    return pl.pallas_call(
        functools.partial(finish_kernel, degrees),
        out_shape=jax.ShapeDtypeStruct(shape, jnp.float32),
        in_specs=[vmem] * len(parts),
        out_specs=vmem,
        compiler_params=compiler_params(),
        name="finish",
    )(*parts)


def body(
    fourier_cycles,
    legendre,
    cycle_weight,
    matched_filter_weights,
    cluster_cycles,
    cluster_flux,
    order_per_slot,
):
    n = lax.axis_size("blk")
    blocks = legendre.shape[2] // n
    columns = fourier_cycles.shape[2]
    channels = matched_filter_weights.shape[2]
    skies = columns // (2 * channels)
    me = lax.axis_index("blk").reshape(1).astype(jnp.int32)
    weights = jnp.transpose(matched_filter_weights, (1, 2, 0))
    widths = split_degrees(blocks)
    offsets = [sum(widths[:c]) for c in range(len(widths))]

    def send(value, x):
        return lax.ppermute(value, "blk", partner(x, n))

    far = range(2, n)
    sent = []
    for c, (offset, width) in enumerate(zip(offsets, widths)):
        pieces = [(x, offset, width) for x in far]
        if c == 0:
            pieces.append((1, 0, blocks))
        cuts = list(cut(me, legendre, pieces, blocks))
        if c == 0:
            near = send(cuts.pop(), 1)
        sent.append([send(value, x) for value, x in zip(cuts, far)])

    own = inject(me, fourier_cycles, cycle_weight, cluster_cycles, cluster_flux)
    cycles = {0: own}
    bit = n // 2
    while bit:
        for x in list(cycles):
            cycles[x ^ bit] = send(cycles[x], bit)
        bit //= 2
    analysis = prepare([cycles[x] for x in range(n)])
    response = response_rows(me, order_per_slot, weights, skies, columns)

    total = None
    for c, (offset, width) in enumerate(zip(offsets, widths)):
        parts = [(near, offset)] + [(value, 0) for value in sent[c]]
        final = c == len(widths) - 1
        result = chunk(
            me,
            order_per_slot,
            legendre,
            parts,
            analysis,
            weights,
            total,
            response if final else None,
            blocks,
            offset,
            width,
        )
        total = result[0]
    returned = [result[0]] + [send(result[x], x) for x in range(1, n)]
    return finish(returned, fourier_cycles.shape, float(legendre.shape[2]))


def solution(mesh):
    return jax.shard_map(
        body,
        mesh=mesh,
        in_specs=(
            P("order", "blk", None),
            P("order", "blk", None),
            P("blk"),
            P("blk", None, None),
            P("order", None),
            P("order", None, None),
            P("order"),
        ),
        out_specs=P("order", "blk", None),
        check_vma=False,
    )
```

```python
import functools

import jax
import jax.numpy as jnp
from jax import lax
from jax.experimental import pallas as pl
from jax.experimental.pallas import tpu as pltpu
from jax.sharding import PartitionSpec as P

LANES = 128
FREE = pl.CostEstimate(flops=0, bytes_accessed=0, transcendentals=0)
VMEM_LIMIT = 48 * 1024 * 1024


def partner(x, n):
    return [(i, i ^ x) for i in range(n)]


def split_degrees(blocks):
    tiles = blocks // LANES
    if tiles < 24:
        return [blocks]
    widths = [8, tiles - 14, 4, 2]
    return [w * LANES for w in widths]


def in_hbm(*arrays):
    return [pltpu.with_memory_space_constraint(array, pltpu.HBM) for array in arrays]


def halves(value):
    high = value.astype(jnp.bfloat16)
    low = (value - high.astype(jnp.float32)).astype(jnp.bfloat16)
    return high, low


def compiler_params(**kwargs):
    return pltpu.CompilerParams(vmem_limit_bytes=VMEM_LIMIT, **kwargs)


def cut_copies(pieces, blocks, me, legendre_ref, outs, sems):
    copies = []
    for number, (x, offset, width) in enumerate(pieces):
        start = pl.multiple_of((me ^ x) * blocks + offset, LANES)
        copies.append(
            pltpu.make_async_copy(
                legendre_ref.at[:, :, pl.ds(start, width)],
                outs[number].at[:, :, pl.ds(0, width)],
                sems.at[number],
            )
        )
    return copies


def cut_kernel(pieces, blocks, me_ref, legendre_ref, *refs):
    copies = cut_copies(pieces, blocks, me_ref[0], legendre_ref, refs[:-1], refs[-1])
    for copy in copies:
        copy.start()
    for copy in copies:
        copy.wait()


def cut(me, legendre, pieces, blocks):
    orders, rows, _ = legendre.shape
    shapes = [jax.ShapeDtypeStruct((orders, rows, w), jnp.float32) for _, _, w in pieces]
    size = sum(orders * rows * w * 4 for _, _, w in pieces)
    return pl.pallas_call(
        functools.partial(cut_kernel, pieces, blocks),
        out_shape=shapes,
        in_specs=[pl.BlockSpec(memory_space=pltpu.SMEM), pl.BlockSpec(memory_space=pltpu.HBM)],
        out_specs=[pl.BlockSpec(memory_space=pl.ANY)] * len(pieces),
        scratch_shapes=[pltpu.SemaphoreType.DMA((len(pieces),))],
        compiler_params=compiler_params(),
        cost_estimate=pl.CostEstimate(flops=0, bytes_accessed=40 * size, transcendentals=0),
        name="cut",
    )(me, *in_hbm(legendre))


def open_kernel(
    pieces, blocks, me_ref, legendre_ref, cycles_ref, weight_ref, hits_ref, flux_ref, *refs
):
    count = len(pieces)
    outs, own_ref = refs[:count], refs[count]
    cycles, weight, hit_cycles, flux, sems, small_sems = refs[count + 1 :]
    orders, rows, columns = cycles.shape
    clusters = flux.shape[1]
    small = [
        pltpu.make_async_copy(source, target, small_sems.at[number])
        for number, (source, target) in enumerate(
            [(cycles_ref, cycles), (weight_ref, weight), (hits_ref, hit_cycles), (flux_ref, flux)]
        )
    ]
    copies = cut_copies(pieces, blocks, me_ref[0], legendre_ref, outs, sems)
    for copy in small + copies:
        copy.start()
    for copy in small:
        copy.wait()
    eye = lax.broadcasted_iota(jnp.int32, (rows, rows), 0) == lax.broadcasted_iota(
        jnp.int32, (rows, rows), 1
    )
    weight_column = jnp.sum(jnp.where(eye, weight[...], 0.0), axis=1, keepdims=True)
    ids = me_ref[0] * rows + lax.broadcasted_iota(jnp.int32, (rows, clusters), 0)
    for k in range(orders):
        hits = (ids == hit_cycles[k : k + 1, :]).astype(jnp.float32)
        added = jnp.dot(
            hits,
            flux[k],
            precision=lax.Precision.HIGHEST,
            preferred_element_type=jnp.float32,
        )
        own_ref[k] = weight_column * (cycles[k] + added)
    tail = pltpu.make_async_copy(
        own_ref, outs[0].at[:, :, pl.ds(pieces[0][2], columns)], small_sems.at[0]
    )
    tail.start()
    for copy in copies + [tail]:
        copy.wait()


def open_blocks(me, legendre, cycles, weight, cluster_cycles, flux, pieces, blocks):
    orders, rows, columns = cycles.shape
    shapes = [jax.ShapeDtypeStruct((orders, rows, w), jnp.float32) for _, _, w in pieces]
    shapes[0] = jax.ShapeDtypeStruct((orders, rows, pieces[0][2] + columns), jnp.float32)
    shapes.append(jax.ShapeDtypeStruct(cycles.shape, jnp.float32))
    size = sum(orders * rows * w * 4 for _, _, w in pieces)
    hbm = pl.BlockSpec(memory_space=pltpu.HBM)
    weight = weight.reshape(1, -1)
    return pl.pallas_call(
        functools.partial(open_kernel, pieces, blocks),
        out_shape=shapes,
        in_specs=[pl.BlockSpec(memory_space=pltpu.SMEM)] + [hbm] * 5,
        out_specs=[pl.BlockSpec(memory_space=pl.ANY)] * len(pieces)
        + [pl.BlockSpec(memory_space=pltpu.VMEM)],
        scratch_shapes=[
            pltpu.VMEM(cycles.shape, jnp.float32),
            pltpu.VMEM(weight.shape, jnp.float32),
            pltpu.VMEM(cluster_cycles.shape, jnp.int32),
            pltpu.VMEM(flux.shape, jnp.float32),
            pltpu.SemaphoreType.DMA((len(pieces),)),
            pltpu.SemaphoreType.DMA((4,)),
        ],
        compiler_params=compiler_params(),
        cost_estimate=FREE,
        name="open",
    )(me, *in_hbm(legendre, cycles, weight, cluster_cycles, flux))


def response_kernel(blocks, scales, skies, me_ref, order_ref, weights_ref, out_ref):
    orders = order_ref.shape[0]
    degree = me_ref[0] * blocks + lax.broadcasted_iota(jnp.int32, (1, blocks), 1)
    factor = 2.0 * degree.astype(jnp.float32) + 1.0
    squares = jnp.concatenate(
        [
            jnp.sum(weights_ref[s] * weights_ref[s], axis=0, keepdims=True) * factor
            for s in range(scales)
        ],
        axis=0,
    )
    columns = out_ref.shape[1]
    scale_of = (lax.broadcasted_iota(jnp.int32, (scales, columns), 1) // skies) % scales
    chosen = scale_of == lax.broadcasted_iota(jnp.int32, (scales, columns), 0)
    out_ref[...] = jnp.zeros_like(out_ref)
    for k in range(orders):
        total = jnp.sum(jnp.where(degree >= order_ref[k], squares, 0.0), axis=1, keepdims=True)
        out_ref[k : k + 1, :] = jnp.sum(jnp.where(chosen, total, 0.0), axis=0, keepdims=True)


def response_rows(me, order_per_slot, weights, skies, columns):
    scales, _, blocks = weights.shape
    smem = pl.BlockSpec(memory_space=pltpu.SMEM)
    vmem = pl.BlockSpec(memory_space=pltpu.VMEM)
    rows = -(-order_per_slot.shape[0] // 8) * 8
    return pl.pallas_call(
        functools.partial(response_kernel, blocks, scales, skies),
        out_shape=jax.ShapeDtypeStruct((rows, columns), jnp.float32),
        in_specs=[smem, smem, vmem],
        out_specs=vmem,
        compiler_params=compiler_params(),
        cost_estimate=FREE,
        name="response",
    )(me, order_per_slot, weights)


def prepare_kernel(*refs):
    pieces, out_ref = refs[:-1], refs[-1]
    for k in range(out_ref.shape[0]):
        whole = jnp.concatenate([piece[k] for piece in pieces], axis=0).T
        high, low = halves(whole)
        out_ref[k] = jnp.concatenate([high, low, high], axis=1)


def prepare(pieces):
    orders, rows, columns = pieces[0][0].shape
    count = len(pieces)
    return pl.pallas_call(
        prepare_kernel,
        out_shape=jax.ShapeDtypeStruct((orders, columns, 3 * rows * count), jnp.bfloat16),
        grid=(1,),
        in_specs=[
            pl.BlockSpec((orders, rows, columns), lambda i, block=at // columns: (0, 0, block))
            for _, at in pieces
        ],
        out_specs=pl.BlockSpec((orders, columns, 3 * rows * count), lambda i: (0, 0, 0)),
        compiler_params=compiler_params(),
        cost_estimate=FREE,
        name="prepare",
    )(*[array for array, _ in pieces])


def chunk_kernel(n, first, last, blocks, offset, tile, me_ref, order_ref, *refs):
    legendre = refs[:n]
    analysis_ref, weights_ref = refs[n : n + 2]
    rest = list(refs[n + 2 :])
    before = None if first else rest.pop(0)
    response = rest.pop(0) if last else None
    total = rest.pop()
    step = pl.program_id(0)
    orders, rows, _ = legendre[0].shape
    scales, channels, _ = weights_ref.shape
    columns = analysis_ref.shape[1]
    skies = columns // (2 * channels)
    everything = n * rows

    @pl.when(step == 0)
    def _():
        total[...] = jnp.zeros_like(total)

    degree = (
        me_ref[0] * blocks
        + offset
        + step * tile
        + lax.broadcasted_iota(jnp.int32, (1, tile), 1)
    )
    for k in range(orders):
        values = jnp.concatenate([block[k] for block in legendre], axis=0)
        high, low = halves(values)
        harmonics = jnp.dot(
            analysis_ref[k],
            jnp.concatenate([high, high, low], axis=0),
            preferred_element_type=jnp.float32,
        )
        harmonics = jnp.where(degree >= order_ref[k], harmonics, 0.0)
        matched = []
        for p in range(2):
            for s in range(scales):
                value = None
                for f in range(channels):
                    at = (p * channels + f) * skies
                    term = weights_ref[s, f : f + 1, :] * harmonics[at : at + skies, :]
                    value = term if value is None else value + term
                matched.append(value)
        matched_high, matched_low = halves(jnp.concatenate(matched, axis=0))
        total[k] += lax.dot_general(
            jnp.concatenate([high, low], axis=0),
            jnp.concatenate([matched_high, matched_low], axis=0),
            (((1,), (1,)), ((), ())),
            preferred_element_type=jnp.float32,
        )

    @pl.when(step == pl.num_programs(0) - 1)
    def _():
        wide = total.shape[2] // 2
        for k in range(orders):
            result = (
                (total[k, everything:, wide:] + total[k, everything:, :wide])
                + total[k, :everything, wide:]
            ) + total[k, :everything, :wide]
            if before is not None:
                result = result + before[k]
            if last:
                for x in range(n):
                    rest[x][k * rows : (k + 1) * rows, :] = result[x * rows : (x + 1) * rows, :]
            else:
                rest[0][k] = result
        if last:
            for x in range(n):
                rest[x][orders * rows :, :] = response[...]


def chunk(me, order_per_slot, parts, analysis, weights, before, response, blocks, offset, width):
    n = len(parts)
    orders, rows, _ = parts[0][0].shape
    columns = analysis.shape[1]
    scales, channels, _ = weights.shape
    tile = next(t for t in (512, 384, 256, 128) if width % t == 0 and offset % t == 0 and blocks % t == 0)
    last = response is not None
    first = before is None
    steps = width // tile

    def at(start):
        return pl.BlockSpec((orders, rows, tile), lambda i, me, order: (0, 0, start // tile + i))

    whole = lambda array: pl.BlockSpec(array.shape, lambda i, me, order: (0,) * array.ndim)
    operands = [array for array, _ in parts] + [analysis, weights]
    in_specs = [at(start) for _, start in parts]
    in_specs += [
        whole(analysis),
        pl.BlockSpec((scales, channels, tile), lambda i, me, order: (0, 0, offset // tile + i)),
    ]
    if not first:
        operands.append(before)
        in_specs.append(whole(before))
    if last:
        operands.append(response)
        in_specs.append(whole(response))
        out_shape = [
            jax.ShapeDtypeStruct((orders * rows + response.shape[0], columns), jnp.float32)
        ] * n
    else:
        out_shape = [jax.ShapeDtypeStruct((orders, n * rows, columns), jnp.float32)]
    macs = orders * width * columns * rows * n
    return pl.pallas_call(
        functools.partial(chunk_kernel, n, first, last, blocks, offset, tile),
        out_shape=out_shape,
        grid_spec=pltpu.PrefetchScalarGridSpec(
            num_scalar_prefetch=2,
            grid=(steps,),
            in_specs=in_specs,
            out_specs=[whole(shape) for shape in out_shape],
            scratch_shapes=[pltpu.VMEM((orders, 2 * n * rows, 2 * columns), jnp.float32)],
        ),
        compiler_params=compiler_params(dimension_semantics=("arbitrary",)),
        cost_estimate=FREE,
        name="chunk",
    )(me, order_per_slot, *operands)


def finish_kernel(degrees, *refs):
    parts, out_ref = refs[:-1], refs[-1]
    orders, rows, _ = out_ref.shape
    total = parts[0][...]
    for part in parts[1:]:
        total = total + part[...]
    for k in range(orders):
        at = orders * rows + k
        out_ref[k] = total[k * rows : (k + 1) * rows, :] * (
            degrees / jnp.sqrt(total[at : at + 1, :])
        )


def finish(parts, shape, degrees):
    vmem = pl.BlockSpec(memory_space=pltpu.VMEM)
    return pl.pallas_call(
        functools.partial(finish_kernel, degrees),
        out_shape=jax.ShapeDtypeStruct(shape, jnp.float32),
        in_specs=[vmem] * len(parts),
        out_specs=vmem,
        compiler_params=compiler_params(),
        cost_estimate=FREE,
        name="finish",
    )(*parts)


def body(
    fourier_cycles,
    legendre,
    cycle_weight,
    matched_filter_weights,
    cluster_cycles,
    cluster_flux,
    order_per_slot,
):
    n = lax.axis_size("blk")
    blocks = legendre.shape[2] // n
    columns = fourier_cycles.shape[2]
    channels = matched_filter_weights.shape[2]
    skies = columns // (2 * channels)
    me = lax.axis_index("blk").reshape(1).astype(jnp.int32)
    weights = jnp.transpose(matched_filter_weights, (1, 2, 0))
    widths = split_degrees(blocks)
    offsets = [sum(widths[:c]) for c in range(len(widths))]

    def send(value, x):
        return lax.ppermute(value, "blk", partner(x, n))

    far = range(2, n)
    first = widths[0]
    top = n // 2
    order = [top] + [x for x in far if x != top]
    *cuts, near, own = open_blocks(
        me,
        legendre,
        fourier_cycles,
        cycle_weight,
        cluster_cycles,
        cluster_flux,
        [(x, 0, first) for x in order] + [(1, 0, blocks)],
        blocks,
    )
    sent = [{x: send(value, x) for value, x in zip(cuts, order)}]
    then, _ = lax.optimization_barrier((me, cuts[0]))
    pieces = [(x, at, w) for at, w in zip(offsets[1:], widths[1:]) for x in order]
    *cuts, home = cut(then, legendre, pieces + [(0, 0, blocks)], blocks)
    for c in range(len(widths) - 1):
        sent.append({x: send(value, x) for value, x in zip(cuts[c * (n - 2) :], order)})
    near = send(near, 1)
    for c, offset in enumerate(offsets):
        sent[c] = {x: (value, 0) for x, value in sent[c].items()}
        sent[c][0] = (home, offset)
        sent[c][1] = (near, offset)

    cycles = {0: (own, 0), top: (sent[0][top][0], first)}
    bit = top // 2
    while bit:
        for x in list(cycles):
            value, at = cycles[x]
            cycles[x ^ bit] = (send(value[:, :, at : at + columns], bit), 0)
        bit //= 2
    analysis = prepare([cycles[x] for x in range(n)])
    response = response_rows(me, order_per_slot, weights, skies, columns)

    total = None
    for c, (offset, width) in enumerate(zip(offsets, widths)):
        final = c == len(widths) - 1
        result = chunk(
            me,
            order_per_slot,
            [sent[c][x] for x in range(n)],
            analysis,
            weights,
            total,
            response if final else None,
            blocks,
            offset,
            width,
        )
        total = result[0]
    returned = [result[0]] + [send(result[x], x) for x in range(1, n)]
    return finish(returned, fourier_cycles.shape, float(legendre.shape[2]))


def solution(mesh):
    return jax.shard_map(
        body,
        mesh=mesh,
        in_specs=(
            P("order", "blk", None),
            P("order", "blk", None),
            P("blk"),
            P("blk", None, None),
            P("order", None),
            P("order", None, None),
            P("order"),
        ),
        out_specs=P("order", "blk", None),
        check_vma=False,
    )
```

```python
import functools

import jax
import jax.numpy as jnp
from jax import lax
from jax.experimental import pallas as pl
from jax.experimental.pallas import tpu as pltpu
from jax.sharding import PartitionSpec as P

LANES = 128
FREE = pl.CostEstimate(flops=0, bytes_accessed=0, transcendentals=0)
VMEM_LIMIT = 48 * 1024 * 1024


def partner(x, n):
    return [(i, i ^ x) for i in range(n)]


def split_degrees(blocks):
    tiles = blocks // LANES
    if tiles < 24:
        return [blocks]
    last = 2
    first = (tiles - last) * 5 // 11
    return [w * LANES for w in (first, tiles - first - last, last)]


def in_hbm(*arrays):
    return [pltpu.with_memory_space_constraint(array, pltpu.HBM) for array in arrays]


def halves(value):
    high = value.astype(jnp.bfloat16)
    low = (value - high.astype(jnp.float32)).astype(jnp.bfloat16)
    return high, low


def compiler_params(**kwargs):
    return pltpu.CompilerParams(vmem_limit_bytes=VMEM_LIMIT, **kwargs)


def cut_copies(pieces, blocks, me, legendre_ref, outs, sems):
    copies = []
    for number, (x, offset, width) in enumerate(pieces):
        start = pl.multiple_of((me ^ x) * blocks + offset, LANES)
        copies.append(
            pltpu.make_async_copy(
                legendre_ref.at[:, :, pl.ds(start, width)],
                outs[number].at[:, :, pl.ds(0, width)],
                sems.at[number],
            )
        )
    return copies


def cut_kernel(pieces, blocks, legendre_ref, *refs):
    copies = cut_copies(pieces, blocks, lax.axis_index("blk"), legendre_ref, refs[:-1], refs[-1])
    for copy in copies:
        copy.start()
    for copy in copies:
        copy.wait()


def cut(legendre, pieces, blocks):
    orders, rows, _ = legendre.shape
    shapes = [jax.ShapeDtypeStruct((orders, rows, w), jnp.float32) for _, _, w in pieces]
    size = sum(orders * rows * w * 4 for _, _, w in pieces)
    return pl.pallas_call(
        functools.partial(cut_kernel, pieces, blocks),
        out_shape=shapes,
        in_specs=[pl.BlockSpec(memory_space=pltpu.HBM)],
        out_specs=[pl.BlockSpec(memory_space=pl.ANY)] * len(pieces),
        scratch_shapes=[pltpu.SemaphoreType.DMA((len(pieces),))],
        compiler_params=compiler_params(),
        cost_estimate=pl.CostEstimate(flops=0, bytes_accessed=40 * size, transcendentals=0),
        name="cut",
    )(*in_hbm(legendre))


def open_kernel(
    pieces, carry, blocks, legendre_ref, cycles_ref, weight_ref, hits_ref, flux_ref, *refs
):
    count = len(pieces)
    me = lax.axis_index("blk")
    outs, own_ref = refs[:count], refs[count]
    cycles, weight, hit_cycles, flux, sems, small_sems = refs[count + 1 :]
    orders, rows, columns = cycles.shape
    clusters = flux.shape[1]
    small = [
        pltpu.make_async_copy(source, target, small_sems.at[number])
        for number, (source, target) in enumerate(
            [(cycles_ref, cycles), (weight_ref, weight), (hits_ref, hit_cycles), (flux_ref, flux)]
        )
    ]
    copies = cut_copies(pieces, blocks, me, legendre_ref, outs, sems)
    for copy in small + copies:
        copy.start()
    small[1].wait()
    eye = lax.broadcasted_iota(jnp.int32, (rows, rows), 0) == lax.broadcasted_iota(
        jnp.int32, (rows, rows), 1
    )
    weight_column = jnp.sum(jnp.where(eye, weight[...], 0.0), axis=1, keepdims=True)
    ids = me * rows + lax.broadcasted_iota(jnp.int32, (rows, clusters), 0)
    for copy in small[:1] + small[2:]:
        copy.wait()
    for k in range(orders):
        hits = (ids == hit_cycles[k : k + 1, :]).astype(jnp.bfloat16)
        terms = []
        left = flux[k]
        for _ in range(3):
            terms.append(left.astype(jnp.bfloat16))
            left = left - terms[-1].astype(jnp.float32)
        sums = jnp.dot(
            hits, jnp.concatenate(terms, axis=1), preferred_element_type=jnp.float32
        )
        added = (sums[:, 2 * columns :] + sums[:, columns : 2 * columns]) + sums[:, :columns]
        value = weight_column * (cycles[k] + added)
        own_ref[k] = value
        for i in carry:
            outs[i][k, :, pl.ds(pieces[i][2], columns)] = value
    for copy in copies:
        copy.wait()


def open_blocks(legendre, cycles, weight, cluster_cycles, flux, pieces, carry, blocks):
    orders, rows, columns = cycles.shape
    shapes = [jax.ShapeDtypeStruct((orders, rows, w), jnp.float32) for _, _, w in pieces]
    for i in carry:
        shapes[i] = jax.ShapeDtypeStruct((orders, rows, pieces[i][2] + columns), jnp.float32)
    shapes.append(jax.ShapeDtypeStruct(cycles.shape, jnp.float32))
    size = sum(orders * rows * w * 4 for _, _, w in pieces)
    hbm = pl.BlockSpec(memory_space=pltpu.HBM)
    weight = weight.reshape(1, -1)
    return pl.pallas_call(
        functools.partial(open_kernel, pieces, carry, blocks),
        out_shape=shapes,
        in_specs=[hbm] * 5,
        out_specs=[
            pl.BlockSpec(memory_space=pltpu.VMEM if i in carry else pl.ANY)
            for i in range(len(pieces))
        ]
        + [pl.BlockSpec(memory_space=pltpu.VMEM)],
        scratch_shapes=[
            pltpu.VMEM(cycles.shape, jnp.float32),
            pltpu.VMEM(weight.shape, jnp.float32),
            pltpu.VMEM(cluster_cycles.shape, jnp.int32),
            pltpu.VMEM(flux.shape, jnp.float32),
            pltpu.SemaphoreType.DMA((len(pieces),)),
            pltpu.SemaphoreType.DMA((4,)),
        ],
        compiler_params=compiler_params(),
        cost_estimate=FREE,
        name="open",
    )(*in_hbm(legendre, cycles, weight, cluster_cycles, flux))


def response_kernel(blocks, scales, skies, order_ref, weights_ref, out_ref, limit_ref):
    orders = order_ref.shape[0]
    begin = lax.axis_index("blk") * blocks
    degree = begin + lax.broadcasted_iota(jnp.int32, (1, blocks), 1)
    factor = 2.0 * degree.astype(jnp.float32) + 1.0
    squares = jnp.concatenate(
        [
            jnp.sum(weights_ref[s] * weights_ref[s], axis=0, keepdims=True) * factor
            for s in range(scales)
        ],
        axis=0,
    )
    columns = out_ref.shape[1]
    scale_of = (lax.broadcasted_iota(jnp.int32, (scales, columns), 1) // skies) % scales
    chosen = scale_of == lax.broadcasted_iota(jnp.int32, (scales, columns), 0)
    out_ref[...] = jnp.zeros_like(out_ref)
    limit_ref[...] = jnp.zeros_like(limit_ref)
    for k in range(orders):
        total = jnp.sum(jnp.where(degree >= order_ref[k], squares, 0.0), axis=1, keepdims=True)
        out_ref[k : k + 1, :] = jnp.sum(jnp.where(chosen, total, 0.0), axis=0, keepdims=True)
        limit_ref[k : k + 1, :] = jnp.full((1, LANES), order_ref[k] - begin, jnp.int32)


def response_rows(order_per_slot, weights, skies, columns):
    scales, _, blocks = weights.shape
    smem = pl.BlockSpec(memory_space=pltpu.SMEM)
    vmem = pl.BlockSpec(memory_space=pltpu.VMEM)
    rows = -(-order_per_slot.shape[0] // 8) * 8
    return pl.pallas_call(
        functools.partial(response_kernel, blocks, scales, skies),
        out_shape=[
            jax.ShapeDtypeStruct((rows, columns), jnp.float32),
            jax.ShapeDtypeStruct((rows, LANES), jnp.int32),
        ],
        in_specs=[smem, vmem],
        out_specs=[vmem, vmem],
        compiler_params=compiler_params(),
        cost_estimate=FREE,
        name="response",
    )(order_per_slot, weights)


def prepare_kernel(*refs):
    pieces, out_ref = refs[:-1], refs[-1]
    for k in range(out_ref.shape[0]):
        whole = jnp.concatenate([piece[k] for piece in pieces], axis=0).T
        high, low = halves(whole)
        out_ref[k] = jnp.concatenate([high, low, high], axis=1)


def prepare(pieces):
    orders, rows, columns = pieces[0][0].shape
    count = len(pieces)
    return pl.pallas_call(
        prepare_kernel,
        out_shape=jax.ShapeDtypeStruct((orders, columns, 3 * rows * count), jnp.bfloat16),
        grid=(1,),
        in_specs=[
            pl.BlockSpec((orders, rows, columns), lambda i, block=at // columns: (0, 0, block))
            for _, at in pieces
        ],
        out_specs=pl.BlockSpec((orders, columns, 3 * rows * count), lambda i: (0, 0, 0)),
        compiler_params=compiler_params(),
        cost_estimate=FREE,
        name="prepare",
    )(*[array for array, _ in pieces])


def chunk_kernel(n, first, last, blocks, offset, starts, tiles, limits_ref, *refs):
    legendre = refs[:n]
    analysis_ref, weights_ref = refs[n : n + 2]
    rest = list(refs[n + 2 :])
    before = None if first else rest.pop(0)
    response = rest.pop(0) if last else None
    orders, rows, _ = legendre[0].shape
    scales, channels, _ = weights_ref.shape
    columns = analysis_ref.shape[1]
    skies = columns // (2 * channels)
    everything = n * rows
    totals = [None] * orders

    def begin_of(start):
        if start is None:
            return pl.multiple_of(lax.axis_index("blk") * blocks + offset, LANES)
        return start

    at = 0
    for tile in tiles:
        degree = offset + at + lax.broadcasted_iota(jnp.int32, (1, tile), 1)
        weights = [
            [weights_ref[s, f : f + 1, offset + at : offset + at + tile] for f in range(channels)]
            for s in range(scales)
        ]
        for k in range(orders):
            values = jnp.concatenate(
                [
                    block[k, :, pl.ds(begin_of(start) + at, tile)]
                    for block, start in zip(legendre, starts)
                ],
                axis=0,
            )
            high, low = halves(values)
            harmonics = jnp.dot(
                analysis_ref[k],
                jnp.concatenate([high, high, low], axis=0),
                preferred_element_type=jnp.float32,
            )
            harmonics = jnp.where(degree >= limits_ref[k : k + 1, :1], harmonics, 0.0)
            matched = []
            for p in range(2):
                for s in range(scales):
                    value = None
                    for f in range(channels):
                        begin = (p * channels + f) * skies
                        term = weights[s][f] * harmonics[begin : begin + skies, :]
                        value = term if value is None else value + term
                    matched.append(value)
            matched_high, matched_low = halves(jnp.concatenate(matched, axis=0))
            product = lax.dot_general(
                jnp.concatenate([high, low], axis=0),
                jnp.concatenate([matched_high, matched_low], axis=0),
                (((1,), (1,)), ((), ())),
                preferred_element_type=jnp.float32,
            )
            totals[k] = product if totals[k] is None else totals[k] + product
        at += tile

    for k in range(orders):
        total = totals[k]
        result = (
            (total[everything:, columns:] + total[everything:, :columns])
            + total[:everything, columns:]
        ) + total[:everything, :columns]
        if before is not None:
            result = result + before[k]
        if last:
            for x in range(n):
                rest[x][k * rows : (k + 1) * rows, :] = result[x * rows : (x + 1) * rows, :]
        else:
            rest[0][k] = result
    if last:
        for x in range(n):
            rest[x][orders * rows :, :] = response[...]


def chunk(limits, parts, analysis, weights, before, response, blocks, offset, width):
    n = len(parts)
    orders, rows, _ = parts[0][0].shape
    columns = analysis.shape[1]
    last = response is not None
    first = before is None
    tiles = [2 * LANES] * (width // (2 * LANES)) + [LANES] * (width // LANES % 2)
    operands = [array for array, _ in parts] + [analysis, weights]
    if not first:
        operands.append(before)
    if last:
        operands.append(response)
        out_shape = [
            jax.ShapeDtypeStruct((orders * rows + response.shape[0], columns), jnp.float32)
        ] * n
    else:
        out_shape = [jax.ShapeDtypeStruct((orders, n * rows, columns), jnp.float32)]
    vmem = pl.BlockSpec(memory_space=pltpu.VMEM)
    return pl.pallas_call(
        functools.partial(
            chunk_kernel,
            n,
            first,
            last,
            blocks,
            offset,
            [start for _, start in parts],
            tiles,
        ),
        out_shape=out_shape,
        in_specs=[vmem] * (len(operands) + 1),
        out_specs=[vmem] * len(out_shape),
        compiler_params=compiler_params(),
        cost_estimate=FREE,
        name="chunk",
    )(limits, *operands)


def finish_kernel(degrees, *refs):
    parts, out_ref = refs[:-1], refs[-1]
    orders, rows, _ = out_ref.shape
    total = parts[0][...]
    for part in parts[1:]:
        total = total + part[...]
    for k in range(orders):
        at = orders * rows + k
        out_ref[k] = total[k * rows : (k + 1) * rows, :] * (
            degrees / jnp.sqrt(total[at : at + 1, :])
        )


def finish(parts, shape, degrees):
    vmem = pl.BlockSpec(memory_space=pltpu.VMEM)
    return pl.pallas_call(
        functools.partial(finish_kernel, degrees),
        out_shape=jax.ShapeDtypeStruct(shape, jnp.float32),
        in_specs=[vmem] * len(parts),
        out_specs=vmem,
        compiler_params=compiler_params(),
        cost_estimate=FREE,
        name="finish",
    )(*parts)


def body(
    fourier_cycles,
    legendre,
    cycle_weight,
    matched_filter_weights,
    cluster_cycles,
    cluster_flux,
    order_per_slot,
):
    n = lax.axis_size("blk")
    blocks = legendre.shape[2] // n
    columns = fourier_cycles.shape[2]
    channels = matched_filter_weights.shape[2]
    skies = columns // (2 * channels)
    weights = jnp.transpose(matched_filter_weights, (1, 2, 0))
    widths = split_degrees(blocks)
    offsets = [sum(widths[:c]) for c in range(len(widths))]

    def send(value, x):
        return lax.ppermute(value, "blk", partner(x, n))

    far = range(2, n)
    first = widths[0]
    top = n - 1
    order = [top] + [x for x in far if x != top]
    *cuts, own = open_blocks(
        legendre,
        fourier_cycles,
        cycle_weight,
        cluster_cycles,
        cluster_flux,
        [(x, 0, first) for x in order],
        [0],
        blocks,
    )
    sent = [{x: (send(value, x), 0) for value, x in zip(cuts, order)}]
    then, _ = lax.optimization_barrier((legendre, cuts[0]))
    pieces = [(x, at, w) for at, w in zip(offsets[1:], widths[1:]) for x in order]
    *cuts, home = cut(then, pieces + [(0, 0, blocks)], blocks)
    for c in range(1, len(widths)):
        here = cuts[(c - 1) * len(order) : c * len(order)]
        sent.append({x: (send(value, x), 0) for value, x in zip(here, order)})
    near = send(legendre, 1)
    for c, offset in enumerate(offsets):
        sent[c][0] = (home, offset)
        sent[c][1] = (near, None)

    cycles = {0: (own, 0), top: (sent[0][top][0], first)}
    bit = n // 4
    while bit:
        for x in list(cycles):
            value, at = cycles[x]
            cycles[x ^ bit] = (send(value[:, :, at : at + columns], bit), 0)
        bit //= 2
    analysis = prepare([cycles[x] for x in range(n)])
    response, limits = response_rows(order_per_slot, weights, skies, columns)

    total = None
    for c, (offset, width) in enumerate(zip(offsets, widths)):
        final = c == len(widths) - 1
        result = chunk(
            limits,
            [sent[c][x] for x in range(n)],
            analysis,
            weights,
            total,
            response if final else None,
            blocks,
            offset,
            width,
        )
        total = result[0]
    returned = [result[0]] + [send(result[x], x) for x in list(far) + [1]]
    return finish(returned, fourier_cycles.shape, float(legendre.shape[2]))


def solution(mesh):
    return jax.shard_map(
        body,
        mesh=mesh,
        in_specs=(
            P("order", "blk", None),
            P("order", "blk", None),
            P("blk"),
            P("blk", None, None),
            P("order", None),
            P("order", None, None),
            P("order"),
        ),
        out_specs=P("order", "blk", None),
        check_vma=False,
    )
```

```python
import functools

import jax
import jax.numpy as jnp
from jax import lax
from jax.experimental import pallas as pl
from jax.experimental.pallas import tpu as pltpu
from jax.sharding import PartitionSpec as P

LANES = 128
FREE = pl.CostEstimate(flops=0, bytes_accessed=0, transcendentals=0)
VMEM_LIMIT = 32 * 1024 * 1024


def partner(x, n):
    return [(i, i ^ x) for i in range(n)]


def split_degrees(tiles):
    last = 2
    first = (tiles - last) * 10 // 21
    return [first, tiles - last - first, last]


def in_hbm(*arrays):
    return [pltpu.with_memory_space_constraint(array, pltpu.HBM) for array in arrays]


def halves(value):
    high = value.astype(jnp.bfloat16)
    low = (value - high.astype(jnp.float32)).astype(jnp.bfloat16)
    return high, low


def compiler_params(**kwargs):
    return pltpu.CompilerParams(vmem_limit_bytes=VMEM_LIMIT, **kwargs)


def width_of(piece):
    return sum(width for _, _, width in piece)


def cut_copies(pieces, blocks, me, legendre_ref, outs, sems):
    copies = []
    for piece, out in zip(pieces, outs):
        at = 0
        for x, offset, width in piece:
            start = pl.multiple_of((me ^ x) * blocks + offset, LANES)
            copies.append(
                pltpu.make_async_copy(
                    legendre_ref.at[:, :, pl.ds(start, width)],
                    out.at[:, :, pl.ds(at, width)],
                    sems.at[len(copies)],
                )
            )
            at += width
    return copies


def cut_kernel(pieces, blocks, legendre_ref, *refs):
    copies = cut_copies(pieces, blocks, lax.axis_index("blk"), legendre_ref, refs[:-1], refs[-1])
    for copy in copies:
        copy.start()
    for copy in copies:
        copy.wait()


def cut(legendre, pieces, blocks):
    orders, rows, _ = legendre.shape
    shapes = [jax.ShapeDtypeStruct((orders, rows, width_of(p)), jnp.float32) for p in pieces]
    size = sum(orders * rows * width_of(p) * 4 for p in pieces)
    return pl.pallas_call(
        functools.partial(cut_kernel, pieces, blocks),
        out_shape=shapes,
        in_specs=[pl.BlockSpec(memory_space=pltpu.HBM)],
        out_specs=[pl.BlockSpec(memory_space=pl.ANY)] * len(pieces),
        scratch_shapes=[pltpu.SemaphoreType.DMA((sum(map(len, pieces)),))],
        compiler_params=compiler_params(),
        cost_estimate=pl.CostEstimate(flops=0, bytes_accessed=40 * size, transcendentals=0),
        name="cut",
    )(*in_hbm(legendre))


def open_kernel(
    pieces, carry, blocks, ending, legendre_ref, cycles_ref, weight_ref, hits_ref, flux_ref, filter_ref, *refs
):
    count = len(pieces)
    me = lax.axis_index("blk")
    outs, own_ref = refs[:count], refs[count]
    cycles, weight, hit_cycles, flux, sems, small_sems, filter_sems = refs[count + 1 :]
    orders, rows, columns = cycles.shape
    clusters = flux.shape[1]
    small = [
        pltpu.make_async_copy(source, target, small_sems.at[number])
        for number, (source, target) in enumerate(
            [(cycles_ref, cycles), (weight_ref, weight), (hits_ref, hit_cycles), (flux_ref, flux)]
        )
    ]
    copies = cut_copies(pieces, blocks, me, legendre_ref, outs, sems)
    if ending:
        scales, channels, _ = filter_ref.shape
        for s in range(scales):
            k, row = divmod(s * channels, rows)
            copies.append(
                pltpu.make_async_copy(
                    filter_ref.at[s, :, pl.ds(blocks - ending, ending)],
                    outs[carry[0]].at[
                        k, pl.ds(row, channels), pl.ds(width_of(pieces[carry[0]]) + columns, ending)
                    ],
                    filter_sems.at[s],
                )
            )
    for copy in small + copies:
        copy.start()
    small[1].wait()
    eye = lax.broadcasted_iota(jnp.int32, (rows, rows), 0) == lax.broadcasted_iota(
        jnp.int32, (rows, rows), 1
    )
    weight_column = jnp.sum(jnp.where(eye, weight[...], 0.0), axis=1, keepdims=True)
    ids = me * rows + lax.broadcasted_iota(jnp.int32, (rows, clusters), 0)
    for copy in small[:1] + small[2:]:
        copy.wait()
    for k in range(orders):
        hits = (ids == hit_cycles[k : k + 1, :]).astype(jnp.bfloat16)
        terms = []
        left = flux[k]
        for _ in range(3):
            terms.append(left.astype(jnp.bfloat16))
            left = left - terms[-1].astype(jnp.float32)
        sums = jnp.dot(
            hits, jnp.concatenate(terms, axis=1), preferred_element_type=jnp.float32
        )
        added = (sums[:, 2 * columns :] + sums[:, columns : 2 * columns]) + sums[:, :columns]
        value = weight_column * (cycles[k] + added)
        own_ref[k] = value
        for i in carry:
            outs[i][k, :, pl.ds(width_of(pieces[i]), columns)] = value
    for copy in copies:
        copy.wait()


def open_blocks(
    legendre, cycles, weight, cluster_cycles, flux, weights, pieces, carry, blocks, ending
):
    orders, rows, columns = cycles.shape
    shapes = [
        jax.ShapeDtypeStruct((orders, rows, width_of(p) + (columns + ending if i in carry else 0)), jnp.float32)
        for i, p in enumerate(pieces)
    ]
    shapes.append(jax.ShapeDtypeStruct(cycles.shape, jnp.float32))
    size = sum(orders * rows * width_of(p) * 4 for p in pieces)
    hbm = pl.BlockSpec(memory_space=pltpu.HBM)
    weight = weight.reshape(1, -1)
    return pl.pallas_call(
        functools.partial(open_kernel, pieces, carry, blocks, ending),
        out_shape=shapes,
        in_specs=[hbm] * 6,
        out_specs=[
            pl.BlockSpec(memory_space=pltpu.VMEM if i in carry else pl.ANY)
            for i in range(len(pieces))
        ]
        + [pl.BlockSpec(memory_space=pltpu.VMEM)],
        scratch_shapes=[
            pltpu.VMEM(cycles.shape, jnp.float32),
            pltpu.VMEM(weight.shape, jnp.float32),
            pltpu.VMEM(cluster_cycles.shape, jnp.int32),
            pltpu.VMEM(flux.shape, jnp.float32),
            pltpu.SemaphoreType.DMA((sum(map(len, pieces)),)),
            pltpu.SemaphoreType.DMA((4,)),
            pltpu.SemaphoreType.DMA((weights.shape[0],)),
        ],
        compiler_params=compiler_params(),
        cost_estimate=FREE,
        name="open",
    )(*in_hbm(legendre, cycles, weight, cluster_cycles, flux, weights))


def response_kernel(blocks, scales, skies, order_ref, weights_ref, out_ref, limit_ref):
    orders = order_ref.shape[0]
    begin = lax.axis_index("blk") * blocks
    degree = begin + lax.broadcasted_iota(jnp.int32, (1, blocks), 1)
    factor = 2.0 * degree.astype(jnp.float32) + 1.0
    squares = jnp.concatenate(
        [
            jnp.sum(weights_ref[s] * weights_ref[s], axis=0, keepdims=True) * factor
            for s in range(scales)
        ],
        axis=0,
    )
    columns = out_ref.shape[1]
    scale_of = (lax.broadcasted_iota(jnp.int32, (scales, columns), 1) // skies) % scales
    chosen = scale_of == lax.broadcasted_iota(jnp.int32, (scales, columns), 0)
    out_ref[...] = jnp.zeros_like(out_ref)
    limit_ref[...] = jnp.zeros_like(limit_ref)
    for k in range(orders):
        total = jnp.sum(jnp.where(degree >= order_ref[k], squares, 0.0), axis=1, keepdims=True)
        out_ref[k : k + 1, :] = jnp.sum(jnp.where(chosen, total, 0.0), axis=0, keepdims=True)
        limit_ref[k : k + 1, :] = jnp.full((1, LANES), order_ref[k] - begin, jnp.int32)


def response_rows(order_per_slot, weights, skies, columns):
    scales, _, blocks = weights.shape
    smem = pl.BlockSpec(memory_space=pltpu.SMEM)
    vmem = pl.BlockSpec(memory_space=pltpu.VMEM)
    rows = -(-order_per_slot.shape[0] // 8) * 8
    return pl.pallas_call(
        functools.partial(response_kernel, blocks, scales, skies),
        out_shape=[
            jax.ShapeDtypeStruct((rows, columns), jnp.float32),
            jax.ShapeDtypeStruct((rows, LANES), jnp.int32),
        ],
        in_specs=[smem, vmem],
        out_specs=[vmem, vmem],
        compiler_params=compiler_params(),
        cost_estimate=FREE,
        name="response",
    )(order_per_slot, weights)


def prepare_kernel(*refs):
    pieces, out_ref = refs[:-1], refs[-1]
    for k in range(out_ref.shape[0]):
        whole = jnp.concatenate([piece[k] for piece in pieces], axis=0).T
        high, low = halves(whole)
        out_ref[k] = jnp.concatenate([high, low, high], axis=1)


def prepare(pieces):
    orders, rows, columns = pieces[0][0].shape
    count = len(pieces)
    return pl.pallas_call(
        prepare_kernel,
        out_shape=jax.ShapeDtypeStruct((orders, columns, 3 * rows * count), jnp.bfloat16),
        grid=(1,),
        in_specs=[
            pl.BlockSpec((orders, rows, columns), lambda i, block=at // columns: (0, 0, block))
            for _, at in pieces
        ],
        out_specs=pl.BlockSpec((orders, columns, 3 * rows * count), lambda i: (0, 0, 0)),
        compiler_params=compiler_params(),
        cost_estimate=FREE,
        name="prepare",
    )(*[array for array, _ in pieces])


def tile_sum(values, analysis, weights, keep, rows):
    scales, channels = len(weights), len(weights[0])
    columns = analysis.shape[0]
    skies = columns // (2 * channels)
    high, low = halves(values)
    harmonics = jnp.dot(
        analysis,
        jnp.concatenate([high, high, low], axis=0),
        preferred_element_type=jnp.float32,
    )
    harmonics = jnp.where(keep, harmonics, 0.0)
    matched = []
    for p in range(2):
        for s in range(scales):
            value = None
            for f in range(channels):
                begin = (p * channels + f) * skies
                term = weights[s][f] * harmonics[begin : begin + skies, :]
                value = term if value is None else value + term
            matched.append(value)
    matched_high, matched_low = halves(jnp.concatenate(matched, axis=0))
    return lax.dot_general(
        jnp.concatenate([high[:rows], low[:rows]], axis=0),
        jnp.concatenate([matched_high, matched_low], axis=0),
        (((1,), (1,)), ((), ())),
        preferred_element_type=jnp.float32,
    )


def fold(total):
    rows, columns = total.shape[0] // 2, total.shape[1] // 2
    return (
        (total[rows:, columns:] + total[rows:, :columns]) + total[:rows, columns:]
    ) + total[:rows, :columns]


def chunk_kernel(n, first, last, blocks, offset, starts, tiles, limits_ref, *refs):
    legendre = refs[:n]
    analysis_ref, weights_ref = refs[n : n + 2]
    rest = list(refs[n + 2 :])
    before = None if first else rest.pop(0)
    response = rest.pop(0) if last else None
    orders, rows, _ = legendre[0].shape
    scales, channels, _ = weights_ref.shape
    totals = [None] * orders

    def begin_of(start):
        if start is None:
            return pl.multiple_of(lax.axis_index("blk") * blocks + offset, LANES)
        return start

    at = 0
    for tile in tiles:
        degree = offset + at + lax.broadcasted_iota(jnp.int32, (1, tile), 1)
        weights = [
            [weights_ref[s, f : f + 1, offset + at : offset + at + tile] for f in range(channels)]
            for s in range(scales)
        ]
        for k in range(orders):
            values = jnp.concatenate(
                [
                    block[k, :, pl.ds(begin_of(start) + at, tile)]
                    for block, start in zip(legendre, starts)
                ],
                axis=0,
            )
            keep = degree >= limits_ref[k : k + 1, :1]
            product = tile_sum(values, analysis_ref[k], weights, keep, n * rows)
            totals[k] = product if totals[k] is None else totals[k] + product
        at += tile

    for k in range(orders):
        result = fold(totals[k])
        if before is not None:
            result = result + before[k]
        if last:
            for x in range(n):
                rest[x][k * rows : (k + 1) * rows, :] = result[x * rows : (x + 1) * rows, :]
        else:
            rest[0][k] = result
    if last:
        for x in range(n):
            rest[x][orders * rows :, :] = response[...]


def chunk(limits, parts, analysis, weights, before, response, blocks, offset, width):
    n = len(parts)
    orders, rows, _ = parts[0][0].shape
    columns = analysis.shape[1]
    last = response is not None
    first = before is None
    tiles = [2 * LANES] * (width // (2 * LANES)) + [LANES] * (width // LANES % 2)
    operands = [array for array, _ in parts] + [analysis, weights]
    if not first:
        operands.append(before)
    if last:
        operands.append(response)
        out_shape = [
            jax.ShapeDtypeStruct((orders * rows + response.shape[0], columns), jnp.float32)
        ] * n
    else:
        out_shape = [jax.ShapeDtypeStruct((orders, n * rows, columns), jnp.float32)]
    vmem = pl.BlockSpec(memory_space=pltpu.VMEM)
    return pl.pallas_call(
        functools.partial(
            chunk_kernel,
            n,
            first,
            last,
            blocks,
            offset,
            [start for _, start in parts],
            tiles,
        ),
        out_shape=out_shape,
        in_specs=[vmem] * (len(operands) + 1),
        out_specs=[vmem] * len(out_shape),
        compiler_params=compiler_params(),
        cost_estimate=FREE,
        name="chunk",
    )(limits, *operands)


def ends_kernel(n, across, blocks, at, limits_ref, *refs):
    home, near, *others = refs[:n]
    analysis_ref, weights_ref, across_ref, own_in, own_out, near_out = refs[n:]
    orders, rows, both = home.shape
    size = both // 2
    scales, channels, _ = weights_ref.shape
    me = lax.axis_index("blk")
    places = [
        pl.multiple_of((me ^ x) * blocks + blocks - size, LANES) for x in (0, across)
    ]
    degree = blocks - size + lax.broadcasted_iota(jnp.int32, (1, size), 1)
    degree = jnp.concatenate([degree, degree + ((me ^ across) - me) * blocks], axis=1)

    def across_row(index):
        k, row = divmod(index, rows)
        return across_ref[k, row : row + 1, at : at + size]

    weights = [
        [
            jnp.concatenate(
                [weights_ref[s, f : f + 1, blocks - size :], across_row(s * channels + f)], axis=1
            )
            for f in range(channels)
        ]
        for s in range(scales)
    ]
    own_out[...] = own_in[...]
    for k in range(orders):
        beside = jnp.concatenate([near[k, :, pl.ds(place, size)] for place in places], axis=1)
        values = jnp.concatenate([home[k], beside] + [other[k] for other in others], axis=0)
        keep = degree >= limits_ref[k : k + 1, :1]
        result = fold(tile_sum(values, analysis_ref[k], weights, keep, 2 * rows))
        own_out[k * rows : (k + 1) * rows, :] += result[:rows]
        near_out[k * rows : (k + 1) * rows, :] = result[rows:]


def ends(limits, parts, analysis, weights, across_weights, at, own, across, blocks):
    n = len(parts)
    orders, rows, _ = parts[0].shape
    vmem = pl.BlockSpec(memory_space=pltpu.VMEM)
    operands = parts + [analysis, weights, across_weights, own]
    return pl.pallas_call(
        functools.partial(ends_kernel, n, across, blocks, at),
        out_shape=[
            jax.ShapeDtypeStruct(own.shape, own.dtype),
            jax.ShapeDtypeStruct((orders * rows, own.shape[1]), own.dtype),
        ],
        in_specs=[vmem] * (len(operands) + 1),
        out_specs=[vmem] * 2,
        compiler_params=compiler_params(),
        cost_estimate=FREE,
        name="ends",
    )(limits, *operands)


def finish_kernel(degrees, *refs):
    parts, out_ref = refs[:-1], refs[-1]
    orders, rows, _ = out_ref.shape
    for k in range(orders):
        total = sum(part[k * rows : (k + 1) * rows, :] for part in parts)
        at = orders * rows + k
        response = sum(part[at : at + 1, :] for part in parts if part.shape[0] > orders * rows)
        out_ref[k] = total * (degrees / jnp.sqrt(response))


def finish(parts, shape, degrees):
    vmem = pl.BlockSpec(memory_space=pltpu.VMEM)
    return pl.pallas_call(
        functools.partial(finish_kernel, degrees),
        out_shape=jax.ShapeDtypeStruct(shape, jnp.float32),
        in_specs=[vmem] * len(parts),
        out_specs=vmem,
        compiler_params=compiler_params(),
        cost_estimate=FREE,
        name="finish",
    )(*parts)


def body(
    fourier_cycles,
    legendre,
    cycle_weight,
    matched_filter_weights,
    cluster_cycles,
    cluster_flux,
    order_per_slot,
):
    n = lax.axis_size("blk")
    blocks = legendre.shape[2] // n
    columns = fourier_cycles.shape[2]
    channels = matched_filter_weights.shape[2]
    skies = columns // (2 * channels)
    weights = jnp.transpose(matched_filter_weights, (1, 2, 0))
    scales = weights.shape[0]
    orders, rows, _ = fourier_cycles.shape
    far = list(range(2, n))
    across = n - 1
    order = [across] + [x for x in far if x != across]
    tiles = blocks // LANES
    if n == 4 and tiles >= 24 and scales * channels == orders * rows and rows % channels == 0:
        ending = LANES
        widths = [w * LANES for w in split_degrees(tiles - 1)]
    else:
        ending = 0
        widths = [blocks]
    offsets = [sum(widths[:c]) for c in range(len(widths))]

    def send(value, x):
        return lax.ppermute(value, "blk", partner(x, n))

    *cuts, own = open_blocks(
        legendre,
        fourier_cycles,
        cycle_weight,
        cluster_cycles,
        cluster_flux,
        weights,
        [[(x, 0, widths[0])] for x in order],
        [0],
        blocks,
        ending,
    )
    then, _ = lax.optimization_barrier((legendre, cuts[0]))
    pieces = [[(x, at, w)] for at, w in zip(offsets[1:], widths[1:]) for x in order]
    if ending:
        at = blocks - ending
        pieces += [[(x, at, ending), (x ^ across, at, ending)] for x in order + [0]]
    *more, home = cut(then, pieces + [[(0, 0, blocks)]], blocks)
    cuts += more
    sent = []
    for offset in offsets:
        sent.append({x: (send(cuts.pop(0), x), 0) for x in order})
    if ending:
        last_parts = {x: send(cuts.pop(0), x) for x in order}
        (last_parts[0],) = cuts
    near = send(legendre, 1)
    for offset, parts in zip(offsets, sent):
        parts[0] = (home, offset)
        parts[1] = (near, None)

    carrier = sent[0][across][0]
    cycles = {0: (own, 0), across: (carrier, widths[0])}
    bit = n // 4
    while bit:
        for x in list(cycles):
            value, at = cycles[x]
            cycles[x ^ bit] = (send(value[:, :, at : at + columns], bit), 0)
        bit //= 2
    analysis = prepare([cycles[x] for x in range(n)])
    response, limits = response_rows(order_per_slot, weights, skies, columns)

    total = None
    for c, (offset, width) in enumerate(zip(offsets, widths)):
        final = c == len(offsets) - 1
        result = chunk(
            limits,
            [sent[c][x] for x in range(n)],
            analysis,
            weights,
            total,
            response if final else None,
            blocks,
            offset,
            width,
        )
        total = result[0]
    returned = [send(result[x], x) for x in far + [1]]
    own = result[0]
    if ending:
        last_parts[1] = near
        own, beside = ends(
            limits,
            [last_parts[x] for x in range(n)],
            analysis,
            weights,
            carrier,
            widths[0] + columns,
            own,
            across,
            blocks,
        )
        returned.append(send(beside, 1))
    return finish([own] + returned, fourier_cycles.shape, float(legendre.shape[2]))


def solution(mesh):
    return jax.shard_map(
        body,
        mesh=mesh,
        in_specs=(
            P("order", "blk", None),
            P("order", "blk", None),
            P("blk"),
            P("blk", None, None),
            P("order", None),
            P("order", None, None),
            P("order"),
        ),
        out_specs=P("order", "blk", None),
        check_vma=False,
    )
```

```python
import functools

import jax
import jax.numpy as jnp
from jax import lax
from jax.experimental import pallas as pl
from jax.experimental.pallas import tpu as pltpu
from jax.sharding import PartitionSpec as P

LANES = 128
FREE = pl.CostEstimate(flops=0, bytes_accessed=0, transcendentals=0)
VMEM_LIMIT = 32 * 1024 * 1024


def partner(x, n):
    return [(i, i ^ x) for i in range(n)]


def split_degrees(tiles):
    last = 2
    first = (tiles - last) * 11 // 21
    return [first, tiles - last - first, last]


def in_hbm(*arrays):
    return [pltpu.with_memory_space_constraint(array, pltpu.HBM) for array in arrays]


def halves(value):
    high = value.astype(jnp.bfloat16)
    low = (value - high.astype(jnp.float32)).astype(jnp.bfloat16)
    return high, low


def compiler_params(**kwargs):
    return pltpu.CompilerParams(vmem_limit_bytes=VMEM_LIMIT, **kwargs)


def width_of(piece):
    return sum(width for _, _, width in piece)


def cut_copies(pieces, blocks, me, legendre_ref, outs, sems):
    copies = []
    for piece, out in zip(pieces, outs):
        at = 0
        for x, offset, width in piece:
            start = pl.multiple_of((me ^ x) * blocks + offset, LANES)
            copies.append(
                pltpu.make_async_copy(
                    legendre_ref.at[:, :, pl.ds(start, width)],
                    out.at[:, :, pl.ds(at, width)],
                    sems.at[len(copies)],
                )
            )
            at += width
    return copies


def cut_kernel(pieces, blocks, carry, ending, legendre_ref, *refs):
    filter_ref, *outs = refs[:-2] if ending else (None, *refs[:-2])
    copies = cut_copies(pieces, blocks, lax.axis_index("blk"), legendre_ref, outs, refs[-2])
    if ending:
        scales, channels, _ = filter_ref.shape
        rows, at = legendre_ref.shape[1], width_of(pieces[carry])
        for s in range(scales):
            k, row = divmod(s * channels, rows)
            copies.append(
                pltpu.make_async_copy(
                    filter_ref.at[s, :, pl.ds(blocks - ending, ending)],
                    outs[carry].at[k, pl.ds(row, channels), pl.ds(at, ending)],
                    refs[-1].at[s],
                )
            )
    for copy in copies:
        copy.start()
    for copy in copies:
        copy.wait()


def cut(legendre, weights, pieces, blocks, carry, ending):
    orders, rows, _ = legendre.shape
    shapes = [
        jax.ShapeDtypeStruct((orders, rows, width_of(p) + (ending if i == carry else 0)), jnp.float32)
        for i, p in enumerate(pieces)
    ]
    operands = in_hbm(legendre, weights) if ending else in_hbm(legendre)
    size = sum(orders * rows * width_of(p) * 4 for p in pieces)
    return pl.pallas_call(
        functools.partial(cut_kernel, pieces, blocks, carry, ending),
        out_shape=shapes,
        in_specs=[pl.BlockSpec(memory_space=pltpu.HBM)] * len(operands),
        out_specs=[pl.BlockSpec(memory_space=pl.ANY)] * len(pieces),
        scratch_shapes=[
            pltpu.SemaphoreType.DMA((sum(map(len, pieces)),)),
            pltpu.SemaphoreType.DMA((weights.shape[0],)),
        ],
        compiler_params=compiler_params(),
        cost_estimate=pl.CostEstimate(flops=0, bytes_accessed=40 * size, transcendentals=0),
        name="cut",
    )(*operands)


def open_kernel(
    pieces, carry, blocks, legendre_ref, cycles_ref, weight_ref, hits_ref, flux_ref, *refs
):
    count = len(pieces)
    me = lax.axis_index("blk")
    outs, own_ref = refs[:count], refs[count]
    cycles, weight, hit_cycles, flux, sems, small_sems = refs[count + 1 :]
    orders, rows, columns = cycles.shape
    clusters = flux.shape[1]
    small = [
        pltpu.make_async_copy(source, target, small_sems.at[number])
        for number, (source, target) in enumerate(
            [(cycles_ref, cycles), (weight_ref, weight), (hits_ref, hit_cycles), (flux_ref, flux)]
        )
    ]
    copies = cut_copies(pieces, blocks, me, legendre_ref, outs, sems)
    for copy in small + copies:
        copy.start()
    small[1].wait()
    eye = lax.broadcasted_iota(jnp.int32, (rows, rows), 0) == lax.broadcasted_iota(
        jnp.int32, (rows, rows), 1
    )
    weight_column = jnp.sum(jnp.where(eye, weight[...], 0.0), axis=1, keepdims=True)
    ids = me * rows + lax.broadcasted_iota(jnp.int32, (rows, clusters), 0)
    for copy in small[:1] + small[2:]:
        copy.wait()
    for k in range(orders):
        hits = (ids == hit_cycles[k : k + 1, :]).astype(jnp.bfloat16)
        terms = []
        left = flux[k]
        for _ in range(3):
            terms.append(left.astype(jnp.bfloat16))
            left = left - terms[-1].astype(jnp.float32)
        sums = jnp.dot(
            hits, jnp.concatenate(terms, axis=1), preferred_element_type=jnp.float32
        )
        added = (sums[:, 2 * columns :] + sums[:, columns : 2 * columns]) + sums[:, :columns]
        value = weight_column * (cycles[k] + added)
        own_ref[k] = value
        for i in carry:
            outs[i][k, :, pl.ds(width_of(pieces[i]), columns)] = value
    for copy in copies:
        copy.wait()


def open_blocks(legendre, cycles, weight, cluster_cycles, flux, pieces, carry, blocks):
    orders, rows, columns = cycles.shape
    shapes = [
        jax.ShapeDtypeStruct((orders, rows, width_of(p) + (columns if i in carry else 0)), jnp.float32)
        for i, p in enumerate(pieces)
    ]
    shapes.append(jax.ShapeDtypeStruct(cycles.shape, jnp.float32))
    size = sum(orders * rows * width_of(p) * 4 for p in pieces)
    hbm = pl.BlockSpec(memory_space=pltpu.HBM)
    weight = weight.reshape(1, -1)
    return pl.pallas_call(
        functools.partial(open_kernel, pieces, carry, blocks),
        out_shape=shapes,
        in_specs=[hbm] * 5,
        out_specs=[
            pl.BlockSpec(memory_space=pltpu.VMEM if i in carry else pl.ANY)
            for i in range(len(pieces))
        ]
        + [pl.BlockSpec(memory_space=pltpu.VMEM)],
        scratch_shapes=[
            pltpu.VMEM(cycles.shape, jnp.float32),
            pltpu.VMEM(weight.shape, jnp.float32),
            pltpu.VMEM(cluster_cycles.shape, jnp.int32),
            pltpu.VMEM(flux.shape, jnp.float32),
            pltpu.SemaphoreType.DMA((sum(map(len, pieces)),)),
            pltpu.SemaphoreType.DMA((4,)),
        ],
        compiler_params=compiler_params(),
        cost_estimate=FREE,
        name="open",
    )(*in_hbm(legendre, cycles, weight, cluster_cycles, flux))


def response_kernel(blocks, scales, skies, order_ref, weights_ref, out_ref, limit_ref):
    orders = order_ref.shape[0]
    begin = lax.axis_index("blk") * blocks
    degree = begin + lax.broadcasted_iota(jnp.int32, (1, blocks), 1)
    factor = 2.0 * degree.astype(jnp.float32) + 1.0
    squares = jnp.concatenate(
        [
            jnp.sum(weights_ref[s] * weights_ref[s], axis=0, keepdims=True) * factor
            for s in range(scales)
        ],
        axis=0,
    )
    columns = out_ref.shape[1]
    scale_of = (lax.broadcasted_iota(jnp.int32, (scales, columns), 1) // skies) % scales
    chosen = scale_of == lax.broadcasted_iota(jnp.int32, (scales, columns), 0)
    out_ref[...] = jnp.zeros_like(out_ref)
    limit_ref[...] = jnp.zeros_like(limit_ref)
    for k in range(orders):
        total = jnp.sum(jnp.where(degree >= order_ref[k], squares, 0.0), axis=1, keepdims=True)
        out_ref[k : k + 1, :] = jnp.sum(jnp.where(chosen, total, 0.0), axis=0, keepdims=True)
        limit_ref[k : k + 1, :] = jnp.full((1, LANES), order_ref[k] - begin, jnp.int32)


def response_rows(order_per_slot, weights, skies, columns):
    scales, _, blocks = weights.shape
    smem = pl.BlockSpec(memory_space=pltpu.SMEM)
    vmem = pl.BlockSpec(memory_space=pltpu.VMEM)
    rows = -(-order_per_slot.shape[0] // 8) * 8
    return pl.pallas_call(
        functools.partial(response_kernel, blocks, scales, skies),
        out_shape=[
            jax.ShapeDtypeStruct((rows, columns), jnp.float32),
            jax.ShapeDtypeStruct((rows, LANES), jnp.int32),
        ],
        in_specs=[smem, vmem],
        out_specs=[vmem, vmem],
        compiler_params=compiler_params(),
        cost_estimate=FREE,
        name="response",
    )(order_per_slot, weights)


def prepare_kernel(*refs):
    pieces, out_ref = refs[:-1], refs[-1]
    for k in range(out_ref.shape[0]):
        whole = jnp.concatenate([piece[k] for piece in pieces], axis=0).T
        high, low = halves(whole)
        out_ref[k] = jnp.concatenate([high, low, high], axis=1)


def prepare(pieces):
    orders, rows, columns = pieces[0][0].shape
    count = len(pieces)
    return pl.pallas_call(
        prepare_kernel,
        out_shape=jax.ShapeDtypeStruct((orders, columns, 3 * rows * count), jnp.bfloat16),
        grid=(1,),
        in_specs=[
            pl.BlockSpec((orders, rows, columns), lambda i, block=at // columns: (0, 0, block))
            for _, at in pieces
        ],
        out_specs=pl.BlockSpec((orders, columns, 3 * rows * count), lambda i: (0, 0, 0)),
        compiler_params=compiler_params(),
        cost_estimate=FREE,
        name="prepare",
    )(*[array for array, _ in pieces])


def tile_sum(values, analysis, weights, keep, rows):
    scales, channels = len(weights), len(weights[0])
    columns = analysis.shape[0]
    skies = columns // (2 * channels)
    high, low = halves(values)
    harmonics = jnp.dot(
        analysis,
        jnp.concatenate([high, high, low], axis=0),
        preferred_element_type=jnp.float32,
    )
    harmonics = jnp.where(keep, harmonics, 0.0)
    matched = []
    for p in range(2):
        for s in range(scales):
            value = None
            for f in range(channels):
                begin = (p * channels + f) * skies
                term = weights[s][f] * harmonics[begin : begin + skies, :]
                value = term if value is None else value + term
            matched.append(value)
    matched_high, matched_low = halves(jnp.concatenate(matched, axis=0))
    return lax.dot_general(
        jnp.concatenate([high[:rows], low[:rows]], axis=0),
        jnp.concatenate([matched_high, matched_low], axis=0),
        (((1,), (1,)), ((), ())),
        preferred_element_type=jnp.float32,
    )


def fold(total):
    rows, columns = total.shape[0] // 2, total.shape[1] // 2
    return (
        (total[rows:, columns:] + total[rows:, :columns]) + total[:rows, columns:]
    ) + total[:rows, :columns]


def chunk_kernel(n, first, last, blocks, offset, starts, tiles, limits_ref, *refs):
    legendre = refs[:n]
    analysis_ref, weights_ref = refs[n : n + 2]
    rest = list(refs[n + 2 :])
    before = None if first else rest.pop(0)
    response = rest.pop(0) if last else None
    orders, rows, _ = legendre[0].shape
    scales, channels, _ = weights_ref.shape
    totals = [None] * orders

    def begin_of(start):
        if start is None:
            return pl.multiple_of(lax.axis_index("blk") * blocks + offset, LANES)
        return start

    at = 0
    for tile in tiles:
        degree = offset + at + lax.broadcasted_iota(jnp.int32, (1, tile), 1)
        weights = [
            [weights_ref[s, f : f + 1, offset + at : offset + at + tile] for f in range(channels)]
            for s in range(scales)
        ]
        for k in range(orders):
            values = jnp.concatenate(
                [
                    block[k, :, pl.ds(begin_of(start) + at, tile)]
                    for block, start in zip(legendre, starts)
                ],
                axis=0,
            )
            keep = degree >= limits_ref[k : k + 1, :1]
            product = tile_sum(values, analysis_ref[k], weights, keep, n * rows)
            totals[k] = product if totals[k] is None else totals[k] + product
        at += tile

    for k in range(orders):
        result = fold(totals[k])
        if before is not None:
            result = result + before[k]
        if last:
            for x in range(n):
                rest[x][k * rows : (k + 1) * rows, :] = result[x * rows : (x + 1) * rows, :]
        else:
            rest[0][k] = result
    if last:
        for x in range(n):
            rest[x][orders * rows :, :] = response[...]


def chunk(limits, parts, analysis, weights, before, response, blocks, offset, width):
    n = len(parts)
    orders, rows, _ = parts[0][0].shape
    columns = analysis.shape[1]
    last = response is not None
    first = before is None
    tiles = [2 * LANES] * (width // (2 * LANES)) + [LANES] * (width // LANES % 2)
    operands = [array for array, _ in parts] + [analysis, weights]
    if not first:
        operands.append(before)
    if last:
        operands.append(response)
        out_shape = [
            jax.ShapeDtypeStruct((orders * rows + response.shape[0], columns), jnp.float32)
        ] * n
    else:
        out_shape = [jax.ShapeDtypeStruct((orders, n * rows, columns), jnp.float32)]
    vmem = pl.BlockSpec(memory_space=pltpu.VMEM)
    return pl.pallas_call(
        functools.partial(
            chunk_kernel,
            n,
            first,
            last,
            blocks,
            offset,
            [start for _, start in parts],
            tiles,
        ),
        out_shape=out_shape,
        in_specs=[vmem] * (len(operands) + 1),
        out_specs=[vmem] * len(out_shape),
        compiler_params=compiler_params(),
        cost_estimate=FREE,
        name="chunk",
    )(limits, *operands)


def ends_kernel(n, across, blocks, at, limits_ref, *refs):
    home, near, *others = refs[:n]
    analysis_ref, weights_ref, across_ref, own_in, own_out, near_out = refs[n:]
    orders, rows, both = home.shape
    size = both // 2
    scales, channels, _ = weights_ref.shape
    me = lax.axis_index("blk")
    places = [
        pl.multiple_of((me ^ x) * blocks + blocks - size, LANES) for x in (0, across)
    ]
    degree = blocks - size + lax.broadcasted_iota(jnp.int32, (1, size), 1)
    degree = jnp.concatenate([degree, degree + ((me ^ across) - me) * blocks], axis=1)

    def across_row(index):
        k, row = divmod(index, rows)
        return across_ref[k, row : row + 1, at : at + size]

    weights = [
        [
            jnp.concatenate(
                [weights_ref[s, f : f + 1, blocks - size :], across_row(s * channels + f)], axis=1
            )
            for f in range(channels)
        ]
        for s in range(scales)
    ]
    own_out[...] = own_in[...]
    for k in range(orders):
        beside = jnp.concatenate([near[k, :, pl.ds(place, size)] for place in places], axis=1)
        values = jnp.concatenate([home[k], beside] + [other[k] for other in others], axis=0)
        keep = degree >= limits_ref[k : k + 1, :1]
        result = fold(tile_sum(values, analysis_ref[k], weights, keep, 2 * rows))
        own_out[k * rows : (k + 1) * rows, :] += result[:rows]
        near_out[k * rows : (k + 1) * rows, :] = result[rows:]


def ends(limits, parts, analysis, weights, across_weights, at, own, across, blocks):
    n = len(parts)
    orders, rows, _ = parts[0].shape
    vmem = pl.BlockSpec(memory_space=pltpu.VMEM)
    operands = parts + [analysis, weights, across_weights, own]
    return pl.pallas_call(
        functools.partial(ends_kernel, n, across, blocks, at),
        out_shape=[
            jax.ShapeDtypeStruct(own.shape, own.dtype),
            jax.ShapeDtypeStruct((orders * rows, own.shape[1]), own.dtype),
        ],
        in_specs=[vmem] * (len(operands) + 1),
        out_specs=[vmem] * 2,
        compiler_params=compiler_params(),
        cost_estimate=FREE,
        name="ends",
    )(limits, *operands)


def finish_kernel(degrees, *refs):
    parts, out_ref = refs[:-1], refs[-1]
    orders, rows, _ = out_ref.shape
    for k in range(orders):
        total = sum(part[k * rows : (k + 1) * rows, :] for part in parts)
        at = orders * rows + k
        response = sum(part[at : at + 1, :] for part in parts if part.shape[0] > orders * rows)
        out_ref[k] = total * (degrees / jnp.sqrt(response))


def finish(parts, shape, degrees):
    vmem = pl.BlockSpec(memory_space=pltpu.VMEM)
    return pl.pallas_call(
        functools.partial(finish_kernel, degrees),
        out_shape=jax.ShapeDtypeStruct(shape, jnp.float32),
        in_specs=[vmem] * len(parts),
        out_specs=vmem,
        compiler_params=compiler_params(),
        cost_estimate=FREE,
        name="finish",
    )(*parts)


def body(
    fourier_cycles,
    legendre,
    cycle_weight,
    matched_filter_weights,
    cluster_cycles,
    cluster_flux,
    order_per_slot,
):
    n = lax.axis_size("blk")
    blocks = legendre.shape[2] // n
    columns = fourier_cycles.shape[2]
    channels = matched_filter_weights.shape[2]
    skies = columns // (2 * channels)
    weights = jnp.transpose(matched_filter_weights, (1, 2, 0))
    scales = weights.shape[0]
    orders, rows, _ = fourier_cycles.shape
    far = list(range(2, n))
    across = n - 1
    order = [across] + [x for x in far if x != across]
    tiles = blocks // LANES
    if n == 4 and tiles >= 24 and scales * channels == orders * rows and rows % channels == 0:
        ending = LANES
        widths = [w * LANES for w in split_degrees(tiles - 1)]
    else:
        ending = 0
        widths = [blocks]
    offsets = [sum(widths[:c]) for c in range(len(widths))]

    def send(value, x):
        return lax.ppermute(value, "blk", partner(x, n))

    *cuts, own = open_blocks(
        legendre,
        fourier_cycles,
        cycle_weight,
        cluster_cycles,
        cluster_flux,
        [[(across, 0, widths[0])]],
        [0],
        blocks,
    )
    then, _ = lax.optimization_barrier((legendre, cuts[0]))
    pieces = [[(x, at, w)] for at, w in zip(offsets, widths) for x in order][1:]
    if ending:
        at = blocks - ending
        pieces += [[(x, at, ending), (x ^ across, at, ending)] for x in order + [0]]
    carry = [p[0] for p in pieces].index((across, offsets[1], widths[1])) if ending else 0
    *more, home = cut(then, weights, pieces + [[(0, 0, blocks)]], blocks, carry, ending)
    cuts += more
    sent = []
    for offset in offsets:
        sent.append({x: (send(cuts.pop(0), x), 0) for x in order})
    if ending:
        last_parts = {x: send(cuts.pop(0), x) for x in order}
        (last_parts[0],) = cuts
    near = send(legendre, 1)
    for offset, parts in zip(offsets, sent):
        parts[0] = (home, offset)
        parts[1] = (near, None)

    carrier = sent[0][across][0]
    cycles = {0: (own, 0), across: (carrier, widths[0])}
    bit = n // 4
    while bit:
        for x in list(cycles):
            value, at = cycles[x]
            cycles[x ^ bit] = (send(value[:, :, at : at + columns], bit), 0)
        bit //= 2
    analysis = prepare([cycles[x] for x in range(n)])
    response, limits = response_rows(order_per_slot, weights, skies, columns)

    total = None
    for c, (offset, width) in enumerate(zip(offsets, widths)):
        final = c == len(offsets) - 1
        result = chunk(
            limits,
            [sent[c][x] for x in range(n)],
            analysis,
            weights,
            total,
            response if final else None,
            blocks,
            offset,
            width,
        )
        total = result[0]
    returned = [send(result[x], x) for x in far + [1]]
    own = result[0]
    if ending:
        last_parts[1] = near
        own, beside = ends(
            limits,
            [last_parts[x] for x in range(n)],
            analysis,
            weights,
            sent[1][across][0],
            widths[1],
            own,
            across,
            blocks,
        )
        returned.append(send(beside, 1))
    return finish([own] + returned, fourier_cycles.shape, float(legendre.shape[2]))


def solution(mesh):
    return jax.shard_map(
        body,
        mesh=mesh,
        in_specs=(
            P("order", "blk", None),
            P("order", "blk", None),
            P("blk"),
            P("blk", None, None),
            P("order", None),
            P("order", None, None),
            P("order"),
        ),
        out_specs=P("order", "blk", None),
        check_vma=False,
    )
```

```python
import functools

import jax
import jax.numpy as jnp
from jax import lax
from jax.experimental import pallas as pl
from jax.experimental.pallas import tpu as pltpu
from jax.sharding import PartitionSpec as P

LANES = 128
FREE = pl.CostEstimate(flops=0, bytes_accessed=0, transcendentals=0)
VMEM_LIMIT = 32 * 1024 * 1024


def partner(x, n):
    return [(i, i ^ x) for i in range(n)]


def split_degrees(tiles):
    last = 2
    first = (tiles - last) * 11 // 21
    return [first, tiles - last - first, last]


def in_hbm(*arrays):
    return [pltpu.with_memory_space_constraint(array, pltpu.HBM) for array in arrays]


def halves(value):
    high = value.astype(jnp.bfloat16)
    low = (value - high.astype(jnp.float32)).astype(jnp.bfloat16)
    return high, low


def compiler_params(**kwargs):
    return pltpu.CompilerParams(vmem_limit_bytes=VMEM_LIMIT, **kwargs)


def width_of(piece):
    return sum(width for _, _, width in piece)


def cut_copies(pieces, blocks, me, legendre_ref, outs, sems):
    copies = []
    for piece, out in zip(pieces, outs):
        at = 0
        for x, offset, width in piece:
            start = pl.multiple_of((me ^ x) * blocks + offset, LANES)
            copies.append(
                pltpu.make_async_copy(
                    legendre_ref.at[:, :, pl.ds(start, width)],
                    out.at[:, :, pl.ds(at, width)],
                    sems.at[len(copies)],
                )
            )
            at += width
    return copies


def cut_kernel(pieces, blocks, carry, ending, legendre_ref, *refs):
    filter_ref, *outs = refs[:-2] if ending else (None, *refs[:-2])
    copies = cut_copies(pieces, blocks, lax.axis_index("blk"), legendre_ref, outs, refs[-2])
    if ending:
        scales, channels, _ = filter_ref.shape
        rows, at = legendre_ref.shape[1], width_of(pieces[carry])
        for s in range(scales):
            k, row = divmod(s * channels, rows)
            copies.append(
                pltpu.make_async_copy(
                    filter_ref.at[s, :, pl.ds(blocks - ending, ending)],
                    outs[carry].at[k, pl.ds(row, channels), pl.ds(at, ending)],
                    refs[-1].at[s],
                )
            )
    for copy in copies:
        copy.start()
    for copy in copies:
        copy.wait()


def cut(legendre, weights, pieces, blocks, carry, ending):
    orders, rows, _ = legendre.shape
    shapes = [
        jax.ShapeDtypeStruct((orders, rows, width_of(p) + (ending if i == carry else 0)), jnp.float32)
        for i, p in enumerate(pieces)
    ]
    operands = in_hbm(legendre, weights) if ending else in_hbm(legendre)
    size = sum(orders * rows * width_of(p) * 4 for p in pieces)
    return pl.pallas_call(
        functools.partial(cut_kernel, pieces, blocks, carry, ending),
        out_shape=shapes,
        in_specs=[pl.BlockSpec(memory_space=pltpu.HBM)] * len(operands),
        out_specs=[pl.BlockSpec(memory_space=pl.ANY)] * len(pieces),
        scratch_shapes=[
            pltpu.SemaphoreType.DMA((sum(map(len, pieces)),)),
            pltpu.SemaphoreType.DMA((weights.shape[0],)),
        ],
        compiler_params=compiler_params(),
        cost_estimate=pl.CostEstimate(flops=0, bytes_accessed=40 * size, transcendentals=0),
        name="cut",
    )(*operands)


def open_kernel(
    pieces, carry, blocks, legendre_ref, cycles_ref, weight_ref, hits_ref, flux_ref, *refs
):
    count = len(pieces)
    me = lax.axis_index("blk")
    outs, own_ref = refs[:count], refs[count]
    cycles, weight, hit_cycles, flux, sems, small_sems = refs[count + 1 :]
    orders, rows, columns = cycles.shape
    clusters = flux.shape[1]
    small = [
        pltpu.make_async_copy(source, target, small_sems.at[number])
        for number, (source, target) in enumerate(
            [(cycles_ref, cycles), (weight_ref, weight), (hits_ref, hit_cycles), (flux_ref, flux)]
        )
    ]
    copies = cut_copies(pieces, blocks, me, legendre_ref, outs, sems)
    for copy in small + copies:
        copy.start()
    small[1].wait()
    eye = lax.broadcasted_iota(jnp.int32, (rows, rows), 0) == lax.broadcasted_iota(
        jnp.int32, (rows, rows), 1
    )
    weight_column = jnp.sum(jnp.where(eye, weight[...], 0.0), axis=1, keepdims=True)
    ids = me * rows + lax.broadcasted_iota(jnp.int32, (rows, clusters), 0)
    for copy in small[:1] + small[2:]:
        copy.wait()
    for k in range(orders):
        hits = (ids == hit_cycles[k : k + 1, :]).astype(jnp.bfloat16)
        terms = []
        left = flux[k]
        for _ in range(3):
            terms.append(left.astype(jnp.bfloat16))
            left = left - terms[-1].astype(jnp.float32)
        sums = jnp.dot(
            hits, jnp.concatenate(terms, axis=1), preferred_element_type=jnp.float32
        )
        added = (sums[:, 2 * columns :] + sums[:, columns : 2 * columns]) + sums[:, :columns]
        value = weight_column * (cycles[k] + added)
        own_ref[k] = value
        for i in carry:
            outs[i][k, :, pl.ds(width_of(pieces[i]), columns)] = value
    for copy in copies:
        copy.wait()


def open_blocks(legendre, cycles, weight, cluster_cycles, flux, pieces, carry, blocks):
    orders, rows, columns = cycles.shape
    shapes = [
        jax.ShapeDtypeStruct((orders, rows, width_of(p) + (columns if i in carry else 0)), jnp.float32)
        for i, p in enumerate(pieces)
    ]
    shapes.append(jax.ShapeDtypeStruct(cycles.shape, jnp.float32))
    size = sum(orders * rows * width_of(p) * 4 for p in pieces)
    hbm = pl.BlockSpec(memory_space=pltpu.HBM)
    weight = weight.reshape(1, -1)
    return pl.pallas_call(
        functools.partial(open_kernel, pieces, carry, blocks),
        out_shape=shapes,
        in_specs=[hbm] * 5,
        out_specs=[
            pl.BlockSpec(memory_space=pltpu.VMEM if i in carry else pl.ANY)
            for i in range(len(pieces))
        ]
        + [pl.BlockSpec(memory_space=pltpu.VMEM)],
        scratch_shapes=[
            pltpu.VMEM(cycles.shape, jnp.float32),
            pltpu.VMEM(weight.shape, jnp.float32),
            pltpu.VMEM(cluster_cycles.shape, jnp.int32),
            pltpu.VMEM(flux.shape, jnp.float32),
            pltpu.SemaphoreType.DMA((sum(map(len, pieces)),)),
            pltpu.SemaphoreType.DMA((4,)),
        ],
        compiler_params=compiler_params(),
        cost_estimate=FREE,
        name="open",
    )(*in_hbm(legendre, cycles, weight, cluster_cycles, flux))


def response_kernel(blocks, scales, skies, order_ref, weights_ref, out_ref, limit_ref):
    orders = order_ref.shape[0]
    begin = lax.axis_index("blk") * blocks
    degree = begin + lax.broadcasted_iota(jnp.int32, (1, blocks), 1)
    factor = 2.0 * degree.astype(jnp.float32) + 1.0
    squares = jnp.concatenate(
        [
            jnp.sum(weights_ref[s] * weights_ref[s], axis=0, keepdims=True) * factor
            for s in range(scales)
        ],
        axis=0,
    )
    columns = out_ref.shape[1]
    scale_of = (lax.broadcasted_iota(jnp.int32, (scales, columns), 1) // skies) % scales
    chosen = scale_of == lax.broadcasted_iota(jnp.int32, (scales, columns), 0)
    out_ref[...] = jnp.zeros_like(out_ref)
    limit_ref[...] = jnp.zeros_like(limit_ref)
    for k in range(orders):
        total = jnp.sum(jnp.where(degree >= order_ref[k], squares, 0.0), axis=1, keepdims=True)
        out_ref[k : k + 1, :] = jnp.sum(jnp.where(chosen, total, 0.0), axis=0, keepdims=True)
        limit_ref[k : k + 1, :] = jnp.full((1, LANES), order_ref[k] - begin, jnp.int32)


def response_rows(order_per_slot, weights, skies, columns):
    scales, _, blocks = weights.shape
    smem = pl.BlockSpec(memory_space=pltpu.SMEM)
    vmem = pl.BlockSpec(memory_space=pltpu.VMEM)
    rows = -(-order_per_slot.shape[0] // 8) * 8
    return pl.pallas_call(
        functools.partial(response_kernel, blocks, scales, skies),
        out_shape=[
            jax.ShapeDtypeStruct((rows, columns), jnp.float32),
            jax.ShapeDtypeStruct((rows, LANES), jnp.int32),
        ],
        in_specs=[smem, vmem],
        out_specs=[vmem, vmem],
        compiler_params=compiler_params(),
        cost_estimate=FREE,
        name="response",
    )(order_per_slot, weights)


def prepare_kernel(*refs):
    pieces, out_ref = refs[:-1], refs[-1]
    for k in range(out_ref.shape[0]):
        whole = jnp.concatenate([piece[k] for piece in pieces], axis=0).T
        high, low = halves(whole)
        out_ref[k] = jnp.concatenate([high, low, high], axis=1)


def prepare(pieces):
    orders, rows, columns = pieces[0][0].shape
    count = len(pieces)
    return pl.pallas_call(
        prepare_kernel,
        out_shape=jax.ShapeDtypeStruct((orders, columns, 3 * rows * count), jnp.bfloat16),
        grid=(1,),
        in_specs=[
            pl.BlockSpec((orders, rows, columns), lambda i, block=at // columns: (0, 0, block))
            for _, at in pieces
        ],
        out_specs=pl.BlockSpec((orders, columns, 3 * rows * count), lambda i: (0, 0, 0)),
        compiler_params=compiler_params(),
        cost_estimate=FREE,
        name="prepare",
    )(*[array for array, _ in pieces])


def tile_sum(values, analysis, weights, keep, rows, stacked):
    scales, channels = len(weights), len(weights[0])
    columns = analysis.shape[0]
    skies = columns // (2 * channels)
    high, low = halves(values)
    cycles = high.shape[0]
    if stacked:
        terms = jnp.concatenate([analysis[:, :cycles], analysis[:, cycles : 2 * cycles]], axis=0)
        both = jnp.dot(terms, high, preferred_element_type=jnp.float32)
        rest = jnp.dot(analysis[:, :cycles], low, preferred_element_type=jnp.float32)
        harmonics = (rest + both[columns:]) + both[:columns]
    else:
        harmonics = jnp.dot(
            analysis,
            jnp.concatenate([high, high, low], axis=0),
            preferred_element_type=jnp.float32,
        )
    harmonics = jnp.where(keep, harmonics, 0.0)
    matched = []
    for p in range(2):
        for s in range(scales):
            value = None
            for f in range(channels):
                begin = (p * channels + f) * skies
                term = weights[s][f] * harmonics[begin : begin + skies, :]
                value = term if value is None else value + term
            matched.append(value)
    matched_high, matched_low = halves(jnp.concatenate(matched, axis=0))
    return lax.dot_general(
        jnp.concatenate([high[:rows], low[:rows]], axis=0),
        jnp.concatenate([matched_high, matched_low], axis=0),
        (((1,), (1,)), ((), ())),
        preferred_element_type=jnp.float32,
    )


def fold(total):
    rows, columns = total.shape[0] // 2, total.shape[1] // 2
    return (
        (total[rows:, columns:] + total[rows:, :columns]) + total[:rows, columns:]
    ) + total[:rows, :columns]


def chunk_kernel(n, first, last, blocks, offset, starts, tiles, limits_ref, *refs):
    legendre = refs[:n]
    analysis_ref, weights_ref = refs[n : n + 2]
    rest = list(refs[n + 2 :])
    before = None if first else rest.pop(0)
    response = rest.pop(0) if last else None
    orders, rows, _ = legendre[0].shape
    scales, channels, _ = weights_ref.shape
    totals = [None] * orders

    def begin_of(start):
        if start is None:
            return pl.multiple_of(lax.axis_index("blk") * blocks + offset, LANES)
        return start

    at = 0
    for tile in tiles:
        degree = offset + at + lax.broadcasted_iota(jnp.int32, (1, tile), 1)
        weights = [
            [weights_ref[s, f : f + 1, offset + at : offset + at + tile] for f in range(channels)]
            for s in range(scales)
        ]
        for k in range(orders):
            values = jnp.concatenate(
                [
                    block[k, :, pl.ds(begin_of(start) + at, tile)]
                    for block, start in zip(legendre, starts)
                ],
                axis=0,
            )
            keep = degree >= limits_ref[k : k + 1, :1]
            product = tile_sum(values, analysis_ref[k], weights, keep, n * rows, not last)
            totals[k] = product if totals[k] is None else totals[k] + product
        at += tile

    for k in range(orders):
        result = fold(totals[k])
        if before is not None:
            result = result + before[k]
        if last:
            for x in range(n):
                rest[x][k * rows : (k + 1) * rows, :] = result[x * rows : (x + 1) * rows, :]
        else:
            rest[0][k] = result
    if last:
        for x in range(n):
            rest[x][orders * rows :, :] = response[...]


def chunk(limits, parts, analysis, weights, before, response, blocks, offset, width):
    n = len(parts)
    orders, rows, _ = parts[0][0].shape
    columns = analysis.shape[1]
    last = response is not None
    first = before is None
    tiles = [2 * LANES] * (width // (2 * LANES)) + [LANES] * (width // LANES % 2)
    operands = [array for array, _ in parts] + [analysis, weights]
    if not first:
        operands.append(before)
    if last:
        operands.append(response)
        out_shape = [
            jax.ShapeDtypeStruct((orders * rows + response.shape[0], columns), jnp.float32)
        ] * n
    else:
        out_shape = [jax.ShapeDtypeStruct((orders, n * rows, columns), jnp.float32)]
    vmem = pl.BlockSpec(memory_space=pltpu.VMEM)
    return pl.pallas_call(
        functools.partial(
            chunk_kernel,
            n,
            first,
            last,
            blocks,
            offset,
            [start for _, start in parts],
            tiles,
        ),
        out_shape=out_shape,
        in_specs=[vmem] * (len(operands) + 1),
        out_specs=[vmem] * len(out_shape),
        compiler_params=compiler_params(),
        cost_estimate=FREE,
        name="chunk",
    )(limits, *operands)


def ends_kernel(n, across, blocks, at, limits_ref, *refs):
    home, near, *others = refs[:n]
    analysis_ref, weights_ref, across_ref, own_in, own_out, near_out = refs[n:]
    orders, rows, both = home.shape
    size = both // 2
    scales, channels, _ = weights_ref.shape
    me = lax.axis_index("blk")
    places = [
        pl.multiple_of((me ^ x) * blocks + blocks - size, LANES) for x in (0, across)
    ]
    degree = blocks - size + lax.broadcasted_iota(jnp.int32, (1, size), 1)
    degree = jnp.concatenate([degree, degree + ((me ^ across) - me) * blocks], axis=1)

    def across_row(index):
        k, row = divmod(index, rows)
        return across_ref[k, row : row + 1, at : at + size]

    weights = [
        [
            jnp.concatenate(
                [weights_ref[s, f : f + 1, blocks - size :], across_row(s * channels + f)], axis=1
            )
            for f in range(channels)
        ]
        for s in range(scales)
    ]
    own_out[...] = own_in[...]
    for k in range(orders):
        beside = jnp.concatenate([near[k, :, pl.ds(place, size)] for place in places], axis=1)
        values = jnp.concatenate([home[k], beside] + [other[k] for other in others], axis=0)
        keep = degree >= limits_ref[k : k + 1, :1]
        result = fold(tile_sum(values, analysis_ref[k], weights, keep, 2 * rows, False))
        own_out[k * rows : (k + 1) * rows, :] += result[:rows]
        near_out[k * rows : (k + 1) * rows, :] = result[rows:]


def ends(limits, parts, analysis, weights, across_weights, at, own, across, blocks):
    n = len(parts)
    orders, rows, _ = parts[0].shape
    vmem = pl.BlockSpec(memory_space=pltpu.VMEM)
    operands = parts + [analysis, weights, across_weights, own]
    return pl.pallas_call(
        functools.partial(ends_kernel, n, across, blocks, at),
        out_shape=[
            jax.ShapeDtypeStruct(own.shape, own.dtype),
            jax.ShapeDtypeStruct((orders * rows, own.shape[1]), own.dtype),
        ],
        in_specs=[vmem] * (len(operands) + 1),
        out_specs=[vmem] * 2,
        compiler_params=compiler_params(),
        cost_estimate=FREE,
        name="ends",
    )(limits, *operands)


def finish_kernel(degrees, *refs):
    parts, out_ref = refs[:-1], refs[-1]
    orders, rows, _ = out_ref.shape
    for k in range(orders):
        total = sum(part[k * rows : (k + 1) * rows, :] for part in parts)
        at = orders * rows + k
        response = sum(part[at : at + 1, :] for part in parts if part.shape[0] > orders * rows)
        out_ref[k] = total * (degrees / jnp.sqrt(response))


def finish(parts, shape, degrees):
    vmem = pl.BlockSpec(memory_space=pltpu.VMEM)
    return pl.pallas_call(
        functools.partial(finish_kernel, degrees),
        out_shape=jax.ShapeDtypeStruct(shape, jnp.float32),
        in_specs=[vmem] * len(parts),
        out_specs=vmem,
        compiler_params=compiler_params(),
        cost_estimate=FREE,
        name="finish",
    )(*parts)


def body(
    fourier_cycles,
    legendre,
    cycle_weight,
    matched_filter_weights,
    cluster_cycles,
    cluster_flux,
    order_per_slot,
):
    n = lax.axis_size("blk")
    blocks = legendre.shape[2] // n
    columns = fourier_cycles.shape[2]
    channels = matched_filter_weights.shape[2]
    skies = columns // (2 * channels)
    weights = jnp.transpose(matched_filter_weights, (1, 2, 0))
    scales = weights.shape[0]
    orders, rows, _ = fourier_cycles.shape
    far = list(range(2, n))
    across = n - 1
    order = [across] + [x for x in far if x != across]
    tiles = blocks // LANES
    if n == 4 and tiles >= 24 and scales * channels == orders * rows and rows % channels == 0:
        ending = LANES
        widths = [w * LANES for w in split_degrees(tiles - 1)]
    else:
        ending = 0
        widths = [blocks]
    offsets = [sum(widths[:c]) for c in range(len(widths))]

    def send(value, x):
        return lax.ppermute(value, "blk", partner(x, n))

    *cuts, own = open_blocks(
        legendre,
        fourier_cycles,
        cycle_weight,
        cluster_cycles,
        cluster_flux,
        [[(across, 0, widths[0])]],
        [0],
        blocks,
    )
    then, _ = lax.optimization_barrier((legendre, cuts[0]))
    pieces = [[(x, at, w)] for at, w in zip(offsets, widths) for x in order][1:]
    if ending:
        at = blocks - ending
        pieces += [[(x, at, ending), (x ^ across, at, ending)] for x in order + [0]]
    carry = [p[0] for p in pieces].index((across, offsets[1], widths[1])) if ending else 0
    *more, home = cut(then, weights, pieces + [[(0, 0, blocks)]], blocks, carry, ending)
    cuts += more
    sent = []
    for offset in offsets:
        sent.append({x: (send(cuts.pop(0), x), 0) for x in order})
    if ending:
        last_parts = {x: send(cuts.pop(0), x) for x in order}
        (last_parts[0],) = cuts
    near = send(legendre, 1)
    for offset, parts in zip(offsets, sent):
        parts[0] = (home, offset)
        parts[1] = (near, None)

    carrier = sent[0][across][0]
    cycles = {0: (own, 0), across: (carrier, widths[0])}
    bit = n // 4
    while bit:
        for x in list(cycles):
            value, at = cycles[x]
            cycles[x ^ bit] = (send(value[:, :, at : at + columns], bit), 0)
        bit //= 2
    analysis = prepare([cycles[x] for x in range(n)])
    response, limits = response_rows(order_per_slot, weights, skies, columns)

    total = None
    for c, (offset, width) in enumerate(zip(offsets, widths)):
        final = c == len(offsets) - 1
        result = chunk(
            limits,
            [sent[c][x] for x in range(n)],
            analysis,
            weights,
            total,
            response if final else None,
            blocks,
            offset,
            width,
        )
        total = result[0]
    returned = [send(result[x], x) for x in far + [1]]
    own = result[0]
    if ending:
        last_parts[1] = near
        own, beside = ends(
            limits,
            [last_parts[x] for x in range(n)],
            analysis,
            weights,
            sent[1][across][0],
            widths[1],
            own,
            across,
            blocks,
        )
        returned.append(send(beside, 1))
    return finish([own] + returned, fourier_cycles.shape, float(legendre.shape[2]))


def solution(mesh):
    return jax.shard_map(
        body,
        mesh=mesh,
        in_specs=(
            P("order", "blk", None),
            P("order", "blk", None),
            P("blk"),
            P("blk", None, None),
            P("order", None),
            P("order", None, None),
            P("order"),
        ),
        out_specs=P("order", "blk", None),
        check_vma=False,
    )
```

```python
import functools

import jax
import jax.numpy as jnp
from jax import lax
from jax.experimental import pallas as pl
from jax.experimental.pallas import tpu as pltpu
from jax.sharding import PartitionSpec as P

LANES = 128
FREE = pl.CostEstimate(flops=0, bytes_accessed=0, transcendentals=0)
VMEM_LIMIT = 32 * 1024 * 1024


def partner(x, n):
    return [(i, i ^ x) for i in range(n)]


def split_degrees(tiles):
    last = 2
    first = (tiles - last) * 11 // 21
    return [first, tiles - last - first, last]


def in_hbm(*arrays):
    return [pltpu.with_memory_space_constraint(array, pltpu.HBM) for array in arrays]


def halves(value):
    high = value.astype(jnp.bfloat16)
    low = (value - high.astype(jnp.float32)).astype(jnp.bfloat16)
    return high, low


def compiler_params(**kwargs):
    return pltpu.CompilerParams(vmem_limit_bytes=VMEM_LIMIT, **kwargs)


def width_of(piece):
    return sum(width for _, _, width in piece)


def cut_copies(pieces, blocks, me, legendre_ref, outs, sems):
    copies = []
    for piece, out in zip(pieces, outs):
        at = 0
        for x, offset, width in piece:
            start = pl.multiple_of((me ^ x) * blocks + offset, LANES)
            copies.append(
                pltpu.make_async_copy(
                    legendre_ref.at[:, :, pl.ds(start, width)],
                    out.at[:, :, pl.ds(at, width)],
                    sems.at[len(copies)],
                )
            )
            at += width
    return copies


def cut_kernel(pieces, blocks, carry, ending, legendre_ref, *refs):
    filter_ref, *outs = refs[:-2] if ending else (None, *refs[:-2])
    copies = cut_copies(pieces, blocks, lax.axis_index("blk"), legendre_ref, outs, refs[-2])
    if ending:
        scales, channels, _ = filter_ref.shape
        rows, at = legendre_ref.shape[1], width_of(pieces[carry])
        for s in range(scales):
            k, row = divmod(s * channels, rows)
            copies.append(
                pltpu.make_async_copy(
                    filter_ref.at[s, :, pl.ds(blocks - ending, ending)],
                    outs[carry].at[k, pl.ds(row, channels), pl.ds(at, ending)],
                    refs[-1].at[s],
                )
            )
    for copy in copies:
        copy.start()
    for copy in copies:
        copy.wait()


def cut(legendre, weights, pieces, blocks, carry, ending):
    orders, rows, _ = legendre.shape
    shapes = [
        jax.ShapeDtypeStruct((orders, rows, width_of(p) + (ending if i == carry else 0)), jnp.float32)
        for i, p in enumerate(pieces)
    ]
    operands = in_hbm(legendre, weights) if ending else in_hbm(legendre)
    size = sum(orders * rows * width_of(p) * 4 for p in pieces)
    return pl.pallas_call(
        functools.partial(cut_kernel, pieces, blocks, carry, ending),
        out_shape=shapes,
        in_specs=[pl.BlockSpec(memory_space=pltpu.HBM)] * len(operands),
        out_specs=[pl.BlockSpec(memory_space=pl.ANY)] * len(pieces),
        scratch_shapes=[
            pltpu.SemaphoreType.DMA((sum(map(len, pieces)),)),
            pltpu.SemaphoreType.DMA((weights.shape[0],)),
        ],
        compiler_params=compiler_params(),
        cost_estimate=pl.CostEstimate(flops=0, bytes_accessed=40 * size, transcendentals=0),
        name="cut",
    )(*operands)


def open_kernel(
    pieces, carry, blocks, legendre_ref, cycles_ref, weight_ref, hits_ref, flux_ref, *refs
):
    count = len(pieces)
    me = lax.axis_index("blk")
    outs, own_ref = refs[:count], refs[count]
    cycles, weight, hit_cycles, flux, sems, small_sems = refs[count + 1 :]
    orders, rows, columns = cycles.shape
    clusters = flux.shape[1]
    small = [
        pltpu.make_async_copy(source, target, small_sems.at[number])
        for number, (source, target) in enumerate(
            [(cycles_ref, cycles), (weight_ref, weight), (hits_ref, hit_cycles), (flux_ref, flux)]
        )
    ]
    copies = cut_copies(pieces, blocks, me, legendre_ref, outs, sems)
    for copy in small + copies:
        copy.start()
    small[1].wait()
    eye = lax.broadcasted_iota(jnp.int32, (rows, rows), 0) == lax.broadcasted_iota(
        jnp.int32, (rows, rows), 1
    )
    weight_column = jnp.sum(jnp.where(eye, weight[...], 0.0), axis=1, keepdims=True)
    ids = me * rows + lax.broadcasted_iota(jnp.int32, (rows, clusters), 0)
    for copy in small[:1] + small[2:]:
        copy.wait()
    for k in range(orders):
        hits = (ids == hit_cycles[k : k + 1, :]).astype(jnp.bfloat16)
        terms = []
        left = flux[k]
        for _ in range(3):
            terms.append(left.astype(jnp.bfloat16))
            left = left - terms[-1].astype(jnp.float32)
        sums = jnp.dot(
            hits, jnp.concatenate(terms, axis=1), preferred_element_type=jnp.float32
        )
        added = (sums[:, 2 * columns :] + sums[:, columns : 2 * columns]) + sums[:, :columns]
        value = weight_column * (cycles[k] + added)
        own_ref[k] = value
        for i in carry:
            outs[i][k, :, pl.ds(width_of(pieces[i]), columns)] = value
    for copy in copies:
        copy.wait()


def open_blocks(legendre, cycles, weight, cluster_cycles, flux, pieces, carry, blocks):
    orders, rows, columns = cycles.shape
    shapes = [
        jax.ShapeDtypeStruct((orders, rows, width_of(p) + (columns if i in carry else 0)), jnp.float32)
        for i, p in enumerate(pieces)
    ]
    shapes.append(jax.ShapeDtypeStruct(cycles.shape, jnp.float32))
    size = sum(orders * rows * width_of(p) * 4 for p in pieces)
    hbm = pl.BlockSpec(memory_space=pltpu.HBM)
    weight = weight.reshape(1, -1)
    return pl.pallas_call(
        functools.partial(open_kernel, pieces, carry, blocks),
        out_shape=shapes,
        in_specs=[hbm] * 5,
        out_specs=[
            pl.BlockSpec(memory_space=pltpu.VMEM if i in carry else pl.ANY)
            for i in range(len(pieces))
        ]
        + [pl.BlockSpec(memory_space=pltpu.VMEM)],
        scratch_shapes=[
            pltpu.VMEM(cycles.shape, jnp.float32),
            pltpu.VMEM(weight.shape, jnp.float32),
            pltpu.VMEM(cluster_cycles.shape, jnp.int32),
            pltpu.VMEM(flux.shape, jnp.float32),
            pltpu.SemaphoreType.DMA((sum(map(len, pieces)),)),
            pltpu.SemaphoreType.DMA((4,)),
        ],
        compiler_params=compiler_params(),
        cost_estimate=FREE,
        name="open",
    )(*in_hbm(legendre, cycles, weight, cluster_cycles, flux))


def response_kernel(blocks, scales, skies, order_ref, weights_ref, out_ref, limit_ref):
    orders = order_ref.shape[0]
    begin = lax.axis_index("blk") * blocks
    degree = begin + lax.broadcasted_iota(jnp.int32, (1, blocks), 1)
    factor = 2.0 * degree.astype(jnp.float32) + 1.0
    squares = jnp.concatenate(
        [
            jnp.sum(weights_ref[s] * weights_ref[s], axis=0, keepdims=True) * factor
            for s in range(scales)
        ],
        axis=0,
    )
    columns = out_ref.shape[1]
    scale_of = (lax.broadcasted_iota(jnp.int32, (scales, columns), 1) // skies) % scales
    chosen = scale_of == lax.broadcasted_iota(jnp.int32, (scales, columns), 0)
    out_ref[...] = jnp.zeros_like(out_ref)
    limit_ref[...] = jnp.zeros_like(limit_ref)
    for k in range(orders):
        total = jnp.sum(jnp.where(degree >= order_ref[k], squares, 0.0), axis=1, keepdims=True)
        out_ref[k : k + 1, :] = jnp.sum(jnp.where(chosen, total, 0.0), axis=0, keepdims=True)
        limit_ref[k : k + 1, :] = jnp.full((1, LANES), order_ref[k] - begin, jnp.int32)


def response_rows(order_per_slot, weights, skies, columns):
    scales, _, blocks = weights.shape
    smem = pl.BlockSpec(memory_space=pltpu.SMEM)
    vmem = pl.BlockSpec(memory_space=pltpu.VMEM)
    rows = -(-order_per_slot.shape[0] // 8) * 8
    return pl.pallas_call(
        functools.partial(response_kernel, blocks, scales, skies),
        out_shape=[
            jax.ShapeDtypeStruct((rows, columns), jnp.float32),
            jax.ShapeDtypeStruct((rows, LANES), jnp.int32),
        ],
        in_specs=[smem, vmem],
        out_specs=[vmem, vmem],
        compiler_params=compiler_params(),
        cost_estimate=FREE,
        name="response",
    )(order_per_slot, weights)


def prepare_kernel(*refs):
    pieces, out_ref = refs[:-1], refs[-1]
    for k in range(out_ref.shape[0]):
        whole = jnp.concatenate([piece[k] for piece in pieces], axis=0).T
        high, low = halves(whole)
        out_ref[k] = jnp.concatenate([high, low, high], axis=1)


def prepare(pieces):
    orders, rows, columns = pieces[0][0].shape
    count = len(pieces)
    return pl.pallas_call(
        prepare_kernel,
        out_shape=jax.ShapeDtypeStruct((orders, columns, 3 * rows * count), jnp.bfloat16),
        grid=(1,),
        in_specs=[
            pl.BlockSpec((orders, rows, columns), lambda i, block=at // columns: (0, 0, block))
            for _, at in pieces
        ],
        out_specs=pl.BlockSpec((orders, columns, 3 * rows * count), lambda i: (0, 0, 0)),
        compiler_params=compiler_params(),
        cost_estimate=FREE,
        name="prepare",
    )(*[array for array, _ in pieces])


def tile_sum(values, analysis, weights, keep, rows):
    scales, channels = len(weights), len(weights[0])
    columns = analysis.shape[0]
    skies = columns // (2 * channels)
    high, low = halves(values)
    harmonics = jnp.dot(
        analysis,
        jnp.concatenate([high, high, low], axis=0),
        preferred_element_type=jnp.float32,
    )
    harmonics = jnp.where(keep, harmonics, 0.0)
    matched = []
    for p in range(2):
        for s in range(scales):
            value = None
            for f in range(channels):
                begin = (p * channels + f) * skies
                term = weights[s][f] * harmonics[begin : begin + skies, :]
                value = term if value is None else value + term
            matched.append(value)
    matched_high, matched_low = halves(jnp.concatenate(matched, axis=0))
    return lax.dot_general(
        jnp.concatenate([high[rows], low[rows]], axis=0),
        jnp.concatenate([matched_high, matched_low], axis=0),
        (((1,), (1,)), ((), ())),
        preferred_element_type=jnp.float32,
    )


def fold(total):
    rows, columns = total.shape[0] // 2, total.shape[1] // 2
    return (
        (total[rows:, columns:] + total[rows:, :columns]) + total[:rows, columns:]
    ) + total[:rows, :columns]


def chunk_kernel(n, first, last, skip, blocks, offset, starts, tiles, limits_ref, *refs):
    legendre = refs[:n]
    analysis_ref, weights_ref = refs[n : n + 2]
    rest = list(refs[n + 2 :])
    before = None if first else rest.pop(0)
    response = rest.pop(0) if last else None
    orders, rows, _ = legendre[0].shape
    scales, channels, _ = weights_ref.shape
    totals = [None] * orders

    def begin_of(start):
        if start is None:
            return pl.multiple_of(lax.axis_index("blk") * blocks + offset, LANES)
        return start

    at = 0
    for tile in tiles:
        degree = offset + at + lax.broadcasted_iota(jnp.int32, (1, tile), 1)
        weights = [
            [weights_ref[s, f : f + 1, offset + at : offset + at + tile] for f in range(channels)]
            for s in range(scales)
        ]
        for k in range(orders):
            values = jnp.concatenate(
                [
                    block[k, :, pl.ds(begin_of(start) + at, tile)]
                    for block, start in zip(legendre, starts)
                ],
                axis=0,
            )
            keep = degree >= limits_ref[k : k + 1, :1]
            product = tile_sum(values, analysis_ref[k], weights, keep, slice(skip * rows, n * rows))
            totals[k] = product if totals[k] is None else totals[k] + product
        at += tile

    for k in range(orders):
        result = fold(totals[k])
        if before is not None:
            result = result + before[k, skip * rows :]
        if skip:
            result = jnp.concatenate([before[k, : skip * rows], result], axis=0)
        if last:
            for x in range(n):
                rest[x][k * rows : (k + 1) * rows, :] = result[x * rows : (x + 1) * rows, :]
        else:
            rest[0][k] = result
    if last:
        for x in range(n):
            rest[x][orders * rows :, :] = response[...]


def chunk(limits, parts, analysis, weights, before, response, blocks, offset, width, skip):
    n = len(parts)
    orders, rows, _ = parts[0][0].shape
    columns = analysis.shape[1]
    last = response is not None
    first = before is None
    tiles = [2 * LANES] * (width // (2 * LANES)) + [LANES] * (width // LANES % 2)
    operands = [array for array, _ in parts] + [analysis, weights]
    if not first:
        operands.append(before)
    if last:
        operands.append(response)
        out_shape = [
            jax.ShapeDtypeStruct((orders * rows + response.shape[0], columns), jnp.float32)
        ] * n
    else:
        out_shape = [jax.ShapeDtypeStruct((orders, n * rows, columns), jnp.float32)]
    vmem = pl.BlockSpec(memory_space=pltpu.VMEM)
    return pl.pallas_call(
        functools.partial(
            chunk_kernel,
            n,
            first,
            last,
            skip,
            blocks,
            offset,
            [start for _, start in parts],
            tiles,
        ),
        out_shape=out_shape,
        in_specs=[vmem] * (len(operands) + 1),
        out_specs=[vmem] * len(out_shape),
        compiler_params=compiler_params(),
        cost_estimate=FREE,
        name="chunk",
    )(limits, *operands)


def ends_kernel(n, across, blocks, at, offset, width, starts, limits_ref, *refs):
    last, refs = refs[:n], refs[n:]
    home, near, *others = refs[:n]
    analysis_ref, weights_ref, across_ref, own_in, own_out, near_out = refs[n:]
    orders, rows, both = home.shape
    size = both // 2
    scales, channels, _ = weights_ref.shape
    me = lax.axis_index("blk")
    places = [
        pl.multiple_of((me ^ x) * blocks + blocks - size, LANES) for x in (0, across)
    ]
    degree = blocks - size + lax.broadcasted_iota(jnp.int32, (1, size), 1)
    degree = jnp.concatenate([degree, degree + ((me ^ across) - me) * blocks], axis=1)

    def across_row(index):
        k, row = divmod(index, rows)
        return across_ref[k, row : row + 1, at : at + size]

    weights = [
        [
            jnp.concatenate(
                [weights_ref[s, f : f + 1, blocks - size :], across_row(s * channels + f)], axis=1
            )
            for f in range(channels)
        ]
        for s in range(scales)
    ]
    last_degree = offset + lax.broadcasted_iota(jnp.int32, (1, width), 1)
    last_weights = [
        [weights_ref[s, f : f + 1, offset : offset + width] for f in range(channels)]
        for s in range(scales)
    ]
    begins = [pl.multiple_of(me * blocks + offset, LANES) if b is None else b for b in starts]
    own_out[...] = own_in[...]
    for k in range(orders):
        beside = jnp.concatenate([near[k, :, pl.ds(place, size)] for place in places], axis=1)
        values = jnp.concatenate([home[k], beside] + [other[k] for other in others], axis=0)
        keep = degree >= limits_ref[k : k + 1, :1]
        total = tile_sum(values, analysis_ref[k], weights, keep, slice(0, 2 * rows))
        values = jnp.concatenate(
            [block[k, :, pl.ds(begin, width)] for block, begin in zip(last, begins)], axis=0
        )
        keep = last_degree >= limits_ref[k : k + 1, :1]
        total += tile_sum(values, analysis_ref[k], last_weights, keep, slice(0, 2 * rows))
        result = fold(total)
        own_out[k * rows : (k + 1) * rows, :] += result[:rows]
        near_out[k * rows : (k + 1) * rows, :] = result[rows:]


def ends(limits, last, parts, analysis, weights, across_weights, at, own, across, blocks, offset, width):
    n = len(parts)
    orders, rows, _ = parts[0].shape
    vmem = pl.BlockSpec(memory_space=pltpu.VMEM)
    operands = [array for array, _ in last] + parts + [analysis, weights, across_weights, own]
    return pl.pallas_call(
        functools.partial(
            ends_kernel, n, across, blocks, at, offset, width, [start for _, start in last]
        ),
        out_shape=[
            jax.ShapeDtypeStruct(own.shape, own.dtype),
            jax.ShapeDtypeStruct((orders * rows, own.shape[1]), own.dtype),
        ],
        in_specs=[vmem] * (len(operands) + 1),
        out_specs=[vmem] * 2,
        compiler_params=compiler_params(),
        cost_estimate=FREE,
        name="ends",
    )(limits, *operands)


def finish_kernel(degrees, *refs):
    parts, out_ref = refs[:-1], refs[-1]
    orders, rows, _ = out_ref.shape
    for k in range(orders):
        total = sum(part[k * rows : (k + 1) * rows, :] for part in parts)
        at = orders * rows + k
        response = sum(part[at : at + 1, :] for part in parts if part.shape[0] > orders * rows)
        out_ref[k] = total * (degrees / jnp.sqrt(response))


def finish(parts, shape, degrees):
    vmem = pl.BlockSpec(memory_space=pltpu.VMEM)
    return pl.pallas_call(
        functools.partial(finish_kernel, degrees),
        out_shape=jax.ShapeDtypeStruct(shape, jnp.float32),
        in_specs=[vmem] * len(parts),
        out_specs=vmem,
        compiler_params=compiler_params(),
        cost_estimate=FREE,
        name="finish",
    )(*parts)


def body(
    fourier_cycles,
    legendre,
    cycle_weight,
    matched_filter_weights,
    cluster_cycles,
    cluster_flux,
    order_per_slot,
):
    n = lax.axis_size("blk")
    blocks = legendre.shape[2] // n
    columns = fourier_cycles.shape[2]
    channels = matched_filter_weights.shape[2]
    skies = columns // (2 * channels)
    weights = jnp.transpose(matched_filter_weights, (1, 2, 0))
    scales = weights.shape[0]
    orders, rows, _ = fourier_cycles.shape
    far = list(range(2, n))
    across = n - 1
    order = [across] + [x for x in far if x != across]
    tiles = blocks // LANES
    if n == 4 and tiles >= 24 and scales * channels == orders * rows and rows % channels == 0:
        ending = LANES
        widths = [w * LANES for w in split_degrees(tiles - 1)]
    else:
        ending = 0
        widths = [blocks]
    offsets = [sum(widths[:c]) for c in range(len(widths))]

    def send(value, x):
        return lax.ppermute(value, "blk", partner(x, n))

    *cuts, own = open_blocks(
        legendre,
        fourier_cycles,
        cycle_weight,
        cluster_cycles,
        cluster_flux,
        [[(across, 0, widths[0])]],
        [0],
        blocks,
    )
    then, _ = lax.optimization_barrier((legendre, cuts[0]))
    pieces = [[(x, at, w)] for at, w in zip(offsets, widths) for x in order][1:]
    if ending:
        at = blocks - ending
        pieces += [[(x, at, ending), (x ^ across, at, ending)] for x in order + [0]]
    carry = [p[0] for p in pieces].index((across, offsets[1], widths[1])) if ending else 0
    *more, home = cut(then, weights, pieces + [[(0, 0, blocks)]], blocks, carry, ending)
    cuts += more
    sent = []
    for offset in offsets:
        sent.append({x: (send(cuts.pop(0), x), 0) for x in order})
    if ending:
        last_parts = {x: send(cuts.pop(0), x) for x in order}
        (last_parts[0],) = cuts
    near = send(legendre, 1)
    for offset, parts in zip(offsets, sent):
        parts[0] = (home, offset)
        parts[1] = (near, None)

    carrier = sent[0][across][0]
    cycles = {0: (own, 0), across: (carrier, widths[0])}
    bit = n // 4
    while bit:
        for x in list(cycles):
            value, at = cycles[x]
            cycles[x ^ bit] = (send(value[:, :, at : at + columns], bit), 0)
        bit //= 2
    analysis = prepare([cycles[x] for x in range(n)])
    response, limits = response_rows(order_per_slot, weights, skies, columns)

    total = None
    for c, (offset, width) in enumerate(zip(offsets, widths)):
        final = c == len(offsets) - 1
        result = chunk(
            limits,
            [sent[c][x] for x in range(n)],
            analysis,
            weights,
            total,
            response if final else None,
            blocks,
            offset,
            width,
            2 if final and ending else 0,
        )
        total = result[0]
    returned = [send(result[x], x) for x in far + [1]]
    own = result[0]
    if ending:
        last_parts[1] = near
        own, beside = ends(
            limits,
            [sent[-1][x] for x in range(n)],
            [last_parts[x] for x in range(n)],
            analysis,
            weights,
            sent[1][across][0],
            widths[1],
            own,
            across,
            blocks,
            offsets[-1],
            widths[-1],
        )
        returned.append(send(beside, 1))
    return finish([own] + returned, fourier_cycles.shape, float(legendre.shape[2]))


def solution(mesh):
    return jax.shard_map(
        body,
        mesh=mesh,
        in_specs=(
            P("order", "blk", None),
            P("order", "blk", None),
            P("blk"),
            P("blk", None, None),
            P("order", None),
            P("order", None, None),
            P("order"),
        ),
        out_specs=P("order", "blk", None),
        check_vma=False,
    )
```

```python
import functools

import jax
import jax.numpy as jnp
from jax import lax
from jax.experimental import pallas as pl
from jax.experimental.pallas import tpu as pltpu
from jax.sharding import PartitionSpec as P

LANES = 128
FREE = pl.CostEstimate(flops=0, bytes_accessed=0, transcendentals=0)
VMEM_LIMIT = 32 * 1024 * 1024


def partner(x, n):
    return [(i, i ^ x) for i in range(n)]


def split_degrees(tiles):
    last = 2
    first = (tiles - last) * 11 // 21
    return [first, tiles - last - first, last]


def in_hbm(*arrays):
    return [pltpu.with_memory_space_constraint(array, pltpu.HBM) for array in arrays]


def halves(value):
    high = value.astype(jnp.bfloat16)
    low = (value - high.astype(jnp.float32)).astype(jnp.bfloat16)
    return high, low


def compiler_params(**kwargs):
    return pltpu.CompilerParams(vmem_limit_bytes=VMEM_LIMIT, **kwargs)


def width_of(piece):
    return sum(width for _, _, width in piece)


def cut_copies(pieces, blocks, me, legendre_ref, outs, sems):
    copies = []
    for piece, out in zip(pieces, outs):
        at = 0
        for x, offset, width in piece:
            start = pl.multiple_of((me ^ x) * blocks + offset, LANES)
            copies.append(
                pltpu.make_async_copy(
                    legendre_ref.at[:, :, pl.ds(start, width)],
                    out.at[:, :, pl.ds(at, width)],
                    sems.at[len(copies)],
                )
            )
            at += width
    return copies


def cut_kernel(pieces, blocks, carry, ending, legendre_ref, *refs):
    filter_ref, *outs = refs[:-2] if ending else (None, *refs[:-2])
    copies = cut_copies(pieces, blocks, lax.axis_index("blk"), legendre_ref, outs, refs[-2])
    if ending:
        scales, channels, _ = filter_ref.shape
        rows, at = legendre_ref.shape[1], width_of(pieces[carry])
        for s in range(scales):
            k, row = divmod(s * channels, rows)
            copies.append(
                pltpu.make_async_copy(
                    filter_ref.at[s, :, pl.ds(blocks - ending, ending)],
                    outs[carry].at[k, pl.ds(row, channels), pl.ds(at, ending)],
                    refs[-1].at[s],
                )
            )
    for copy in copies:
        copy.start()
    for copy in copies:
        copy.wait()


def cut(legendre, weights, pieces, blocks, carry, ending):
    orders, rows, _ = legendre.shape
    shapes = [
        jax.ShapeDtypeStruct((orders, rows, width_of(p) + (ending if i == carry else 0)), jnp.float32)
        for i, p in enumerate(pieces)
    ]
    operands = in_hbm(legendre, weights) if ending else in_hbm(legendre)
    size = sum(orders * rows * width_of(p) * 4 for p in pieces)
    return pl.pallas_call(
        functools.partial(cut_kernel, pieces, blocks, carry, ending),
        out_shape=shapes,
        in_specs=[pl.BlockSpec(memory_space=pltpu.HBM)] * len(operands),
        out_specs=[pl.BlockSpec(memory_space=pl.ANY)] * len(pieces),
        scratch_shapes=[
            pltpu.SemaphoreType.DMA((sum(map(len, pieces)),)),
            pltpu.SemaphoreType.DMA((weights.shape[0],)),
        ],
        compiler_params=compiler_params(),
        cost_estimate=pl.CostEstimate(flops=0, bytes_accessed=40 * size, transcendentals=0),
        name="cut",
    )(*operands)


def open_kernel(
    pieces, carry, blocks, legendre_ref, cycles_ref, weight_ref, hits_ref, flux_ref, *refs
):
    count = len(pieces)
    me = lax.axis_index("blk")
    outs, own_ref = refs[:count], refs[count]
    cycles, weight, hit_cycles, flux, sems, small_sems = refs[count + 1 :]
    orders, rows, columns = cycles.shape
    clusters = flux.shape[1]
    small = [
        pltpu.make_async_copy(source, target, small_sems.at[number])
        for number, (source, target) in enumerate(
            [(cycles_ref, cycles), (weight_ref, weight), (hits_ref, hit_cycles), (flux_ref, flux)]
        )
    ]
    copies = cut_copies(pieces, blocks, me, legendre_ref, outs, sems)
    for copy in small + copies:
        copy.start()
    small[1].wait()
    eye = lax.broadcasted_iota(jnp.int32, (rows, rows), 0) == lax.broadcasted_iota(
        jnp.int32, (rows, rows), 1
    )
    weight_column = jnp.sum(jnp.where(eye, weight[...], 0.0), axis=1, keepdims=True)
    ids = me * rows + lax.broadcasted_iota(jnp.int32, (rows, clusters), 0)
    for copy in small[:1] + small[2:]:
        copy.wait()
    for k in range(orders):
        hits = (ids == hit_cycles[k : k + 1, :]).astype(jnp.bfloat16)
        terms = []
        left = flux[k]
        for _ in range(3):
            terms.append(left.astype(jnp.bfloat16))
            left = left - terms[-1].astype(jnp.float32)
        sums = jnp.dot(
            hits, jnp.concatenate(terms, axis=1), preferred_element_type=jnp.float32
        )
        added = (sums[:, 2 * columns :] + sums[:, columns : 2 * columns]) + sums[:, :columns]
        value = weight_column * (cycles[k] + added)
        own_ref[k] = value
        for i in carry:
            outs[i][k, :, pl.ds(width_of(pieces[i]), columns)] = value
    for copy in copies:
        copy.wait()


def open_blocks(legendre, cycles, weight, cluster_cycles, flux, pieces, carry, blocks):
    orders, rows, columns = cycles.shape
    shapes = [
        jax.ShapeDtypeStruct((orders, rows, width_of(p) + (columns if i in carry else 0)), jnp.float32)
        for i, p in enumerate(pieces)
    ]
    shapes.append(jax.ShapeDtypeStruct(cycles.shape, jnp.float32))
    size = sum(orders * rows * width_of(p) * 4 for p in pieces)
    hbm = pl.BlockSpec(memory_space=pltpu.HBM)
    weight = weight.reshape(1, -1)
    return pl.pallas_call(
        functools.partial(open_kernel, pieces, carry, blocks),
        out_shape=shapes,
        in_specs=[hbm] * 5,
        out_specs=[
            pl.BlockSpec(memory_space=pltpu.VMEM if i in carry else pl.ANY)
            for i in range(len(pieces))
        ]
        + [pl.BlockSpec(memory_space=pltpu.VMEM)],
        scratch_shapes=[
            pltpu.VMEM(cycles.shape, jnp.float32),
            pltpu.VMEM(weight.shape, jnp.float32),
            pltpu.VMEM(cluster_cycles.shape, jnp.int32),
            pltpu.VMEM(flux.shape, jnp.float32),
            pltpu.SemaphoreType.DMA((sum(map(len, pieces)),)),
            pltpu.SemaphoreType.DMA((4,)),
        ],
        compiler_params=compiler_params(),
        cost_estimate=FREE,
        name="open",
    )(*in_hbm(legendre, cycles, weight, cluster_cycles, flux))


def response_kernel(blocks, scales, skies, order_ref, weights_ref, out_ref, limit_ref):
    orders = order_ref.shape[0]
    begin = lax.axis_index("blk") * blocks
    degree = begin + lax.broadcasted_iota(jnp.int32, (1, blocks), 1)
    factor = 2.0 * degree.astype(jnp.float32) + 1.0
    squares = jnp.concatenate(
        [
            jnp.sum(weights_ref[s] * weights_ref[s], axis=0, keepdims=True) * factor
            for s in range(scales)
        ],
        axis=0,
    )
    columns = out_ref.shape[1]
    scale_of = (lax.broadcasted_iota(jnp.int32, (scales, columns), 1) // skies) % scales
    chosen = scale_of == lax.broadcasted_iota(jnp.int32, (scales, columns), 0)
    out_ref[...] = jnp.zeros_like(out_ref)
    limit_ref[...] = jnp.zeros_like(limit_ref)
    for k in range(orders):
        total = jnp.sum(jnp.where(degree >= order_ref[k], squares, 0.0), axis=1, keepdims=True)
        out_ref[k : k + 1, :] = jnp.sum(jnp.where(chosen, total, 0.0), axis=0, keepdims=True)
        limit_ref[k : k + 1, :] = jnp.full((1, LANES), order_ref[k] - begin, jnp.int32)


def response_rows(order_per_slot, weights, skies, columns):
    scales, _, blocks = weights.shape
    smem = pl.BlockSpec(memory_space=pltpu.SMEM)
    vmem = pl.BlockSpec(memory_space=pltpu.VMEM)
    rows = -(-order_per_slot.shape[0] // 8) * 8
    return pl.pallas_call(
        functools.partial(response_kernel, blocks, scales, skies),
        out_shape=[
            jax.ShapeDtypeStruct((rows, columns), jnp.float32),
            jax.ShapeDtypeStruct((rows, LANES), jnp.int32),
        ],
        in_specs=[smem, vmem],
        out_specs=[vmem, vmem],
        compiler_params=compiler_params(),
        cost_estimate=FREE,
        name="response",
    )(order_per_slot, weights)


def prepare_kernel(*refs):
    pieces, out_ref = refs[:-1], refs[-1]
    for k in range(out_ref.shape[0]):
        whole = jnp.concatenate([piece[k] for piece in pieces], axis=0).T
        high, low = halves(whole)
        out_ref[k] = jnp.concatenate([high, low, high], axis=1)


def prepare(pieces):
    orders, rows, columns = pieces[0][0].shape
    count = len(pieces)
    return pl.pallas_call(
        prepare_kernel,
        out_shape=jax.ShapeDtypeStruct((orders, columns, 3 * rows * count), jnp.bfloat16),
        grid=(1,),
        in_specs=[
            pl.BlockSpec((orders, rows, columns), lambda i, block=at // columns: (0, 0, block))
            for _, at in pieces
        ],
        out_specs=pl.BlockSpec((orders, columns, 3 * rows * count), lambda i: (0, 0, 0)),
        compiler_params=compiler_params(),
        cost_estimate=FREE,
        name="prepare",
    )(*[array for array, _ in pieces])


def tile_sum(values, analysis, weights, keep, rows, stacked=False):
    scales, channels = len(weights), len(weights[0])
    columns = analysis.shape[0]
    skies = columns // (2 * channels)
    high, low = halves(values)
    cycles = high.shape[0]
    if stacked:
        terms = jnp.concatenate([analysis[:, :cycles], analysis[:, cycles : 2 * cycles]], axis=0)
        both = jnp.dot(terms, high, preferred_element_type=jnp.float32)
        rest = jnp.dot(analysis[:, :cycles], low, preferred_element_type=jnp.float32)
        harmonics = (rest + both[columns:]) + both[:columns]
    else:
        harmonics = jnp.dot(
            analysis,
            jnp.concatenate([high, high, low], axis=0),
            preferred_element_type=jnp.float32,
        )
    harmonics = jnp.where(keep, harmonics, 0.0)
    matched = []
    for p in range(2):
        for s in range(scales):
            value = None
            for f in range(channels):
                begin = (p * channels + f) * skies
                term = weights[s][f] * harmonics[begin : begin + skies, :]
                value = term if value is None else value + term
            matched.append(value)
    matched_high, matched_low = halves(jnp.concatenate(matched, axis=0))
    return lax.dot_general(
        jnp.concatenate([high[rows], low[rows]], axis=0),
        jnp.concatenate([matched_high, matched_low], axis=0),
        (((1,), (1,)), ((), ())),
        preferred_element_type=jnp.float32,
    )


def fold(total):
    rows, columns = total.shape[0] // 2, total.shape[1] // 2
    return (
        (total[rows:, columns:] + total[rows:, :columns]) + total[:rows, columns:]
    ) + total[:rows, :columns]


def chunk_kernel(n, first, last, skip, blocks, offset, starts, tiles, limits_ref, *refs):
    legendre = refs[:n]
    analysis_ref, weights_ref = refs[n : n + 2]
    rest = list(refs[n + 2 :])
    before = None if first else rest.pop(0)
    response = rest.pop(0) if last else None
    orders, rows, _ = legendre[0].shape
    scales, channels, _ = weights_ref.shape
    totals = [None] * orders

    def begin_of(start):
        if start is None:
            return pl.multiple_of(lax.axis_index("blk") * blocks + offset, LANES)
        return start

    at = 0
    for tile in tiles:
        degree = offset + at + lax.broadcasted_iota(jnp.int32, (1, tile), 1)
        weights = [
            [weights_ref[s, f : f + 1, offset + at : offset + at + tile] for f in range(channels)]
            for s in range(scales)
        ]
        for k in range(orders):
            values = jnp.concatenate(
                [
                    block[k, :, pl.ds(begin_of(start) + at, tile)]
                    for block, start in zip(legendre, starts)
                ],
                axis=0,
            )
            keep = degree >= limits_ref[k : k + 1, :1]
            product = tile_sum(values, analysis_ref[k], weights, keep, slice(skip * rows, n * rows), not last)
            totals[k] = product if totals[k] is None else totals[k] + product
        at += tile

    for k in range(orders):
        result = fold(totals[k])
        if before is not None:
            result = result + before[k, skip * rows :]
        if skip:
            result = jnp.concatenate([before[k, : skip * rows], result], axis=0)
        if last:
            for x in range(n):
                rest[x][k * rows : (k + 1) * rows, :] = result[x * rows : (x + 1) * rows, :]
        else:
            rest[0][k] = result
    if last:
        for x in range(n):
            rest[x][orders * rows :, :] = response[...]


def chunk(limits, parts, analysis, weights, before, response, blocks, offset, width, skip):
    n = len(parts)
    orders, rows, _ = parts[0][0].shape
    columns = analysis.shape[1]
    last = response is not None
    first = before is None
    tiles = [2 * LANES] * (width // (2 * LANES)) + [LANES] * (width // LANES % 2)
    operands = [array for array, _ in parts] + [analysis, weights]
    if not first:
        operands.append(before)
    if last:
        operands.append(response)
        out_shape = [
            jax.ShapeDtypeStruct((orders * rows + response.shape[0], columns), jnp.float32)
        ] * n
    else:
        out_shape = [jax.ShapeDtypeStruct((orders, n * rows, columns), jnp.float32)]
    vmem = pl.BlockSpec(memory_space=pltpu.VMEM)
    return pl.pallas_call(
        functools.partial(
            chunk_kernel,
            n,
            first,
            last,
            skip,
            blocks,
            offset,
            [start for _, start in parts],
            tiles,
        ),
        out_shape=out_shape,
        in_specs=[vmem] * (len(operands) + 1),
        out_specs=[vmem] * len(out_shape),
        compiler_params=compiler_params(),
        cost_estimate=FREE,
        name="chunk",
    )(limits, *operands)


def ends_kernel(n, across, blocks, at, offset, width, starts, limits_ref, *refs):
    last, refs = refs[:n], refs[n:]
    home, near, *others = refs[:n]
    analysis_ref, weights_ref, across_ref, own_in, own_out, near_out = refs[n:]
    orders, rows, both = home.shape
    size = both // 2
    scales, channels, _ = weights_ref.shape
    me = lax.axis_index("blk")
    places = [
        pl.multiple_of((me ^ x) * blocks + blocks - size, LANES) for x in (0, across)
    ]
    degree = blocks - size + lax.broadcasted_iota(jnp.int32, (1, size), 1)
    degree = jnp.concatenate([degree, degree + ((me ^ across) - me) * blocks], axis=1)

    def across_row(index):
        k, row = divmod(index, rows)
        return across_ref[k, row : row + 1, at : at + size]

    weights = [
        [
            jnp.concatenate(
                [weights_ref[s, f : f + 1, blocks - size :], across_row(s * channels + f)], axis=1
            )
            for f in range(channels)
        ]
        for s in range(scales)
    ]
    last_degree = offset + lax.broadcasted_iota(jnp.int32, (1, width), 1)
    last_weights = [
        [weights_ref[s, f : f + 1, offset : offset + width] for f in range(channels)]
        for s in range(scales)
    ]
    begins = [pl.multiple_of(me * blocks + offset, LANES) if b is None else b for b in starts]
    own_out[...] = own_in[...]
    for k in range(orders):
        beside = jnp.concatenate([near[k, :, pl.ds(place, size)] for place in places], axis=1)
        values = jnp.concatenate([home[k], beside] + [other[k] for other in others], axis=0)
        keep = degree >= limits_ref[k : k + 1, :1]
        total = tile_sum(values, analysis_ref[k], weights, keep, slice(0, 2 * rows))
        values = jnp.concatenate(
            [block[k, :, pl.ds(begin, width)] for block, begin in zip(last, begins)], axis=0
        )
        keep = last_degree >= limits_ref[k : k + 1, :1]
        total += tile_sum(values, analysis_ref[k], last_weights, keep, slice(0, 2 * rows))
        result = fold(total)
        own_out[k * rows : (k + 1) * rows, :] += result[:rows]
        near_out[k * rows : (k + 1) * rows, :] = result[rows:]


def ends(limits, last, parts, analysis, weights, across_weights, at, own, across, blocks, offset, width):
    n = len(parts)
    orders, rows, _ = parts[0].shape
    vmem = pl.BlockSpec(memory_space=pltpu.VMEM)
    operands = [array for array, _ in last] + parts + [analysis, weights, across_weights, own]
    return pl.pallas_call(
        functools.partial(
            ends_kernel, n, across, blocks, at, offset, width, [start for _, start in last]
        ),
        out_shape=[
            jax.ShapeDtypeStruct(own.shape, own.dtype),
            jax.ShapeDtypeStruct((orders * rows, own.shape[1]), own.dtype),
        ],
        in_specs=[vmem] * (len(operands) + 1),
        out_specs=[vmem] * 2,
        compiler_params=compiler_params(),
        cost_estimate=FREE,
        name="ends",
    )(limits, *operands)


def finish_kernel(degrees, *refs):
    *parts, out_ref, done, sems = refs
    orders, rows, _ = out_ref.shape
    copies = []
    for k in range(orders):
        total = sum(part[k * rows : (k + 1) * rows, :] for part in parts)
        at = orders * rows + k
        response = sum(part[at : at + 1, :] for part in parts if part.shape[0] > orders * rows)
        done[k] = total * (degrees / jnp.sqrt(response))
        copies.append(pltpu.make_async_copy(done.at[k], out_ref.at[k], sems.at[k]))
        copies[-1].start()
    for copy in copies:
        copy.wait()


def finish(parts, shape, degrees):
    vmem = pl.BlockSpec(memory_space=pltpu.VMEM)
    return pl.pallas_call(
        functools.partial(finish_kernel, degrees),
        out_shape=jax.ShapeDtypeStruct(shape, jnp.float32),
        in_specs=[vmem] * len(parts),
        out_specs=pl.BlockSpec(memory_space=pltpu.HBM),
        scratch_shapes=[pltpu.VMEM(shape, jnp.float32), pltpu.SemaphoreType.DMA((shape[0],))],
        compiler_params=compiler_params(),
        cost_estimate=FREE,
        name="finish",
    )(*parts)


def body(
    fourier_cycles,
    legendre,
    cycle_weight,
    matched_filter_weights,
    cluster_cycles,
    cluster_flux,
    order_per_slot,
):
    n = lax.axis_size("blk")
    blocks = legendre.shape[2] // n
    columns = fourier_cycles.shape[2]
    channels = matched_filter_weights.shape[2]
    skies = columns // (2 * channels)
    weights = jnp.transpose(matched_filter_weights, (1, 2, 0))
    scales = weights.shape[0]
    orders, rows, _ = fourier_cycles.shape
    far = list(range(2, n))
    across = n - 1
    order = [across] + [x for x in far if x != across]
    tiles = blocks // LANES
    if n == 4 and tiles >= 24 and scales * channels == orders * rows and rows % channels == 0:
        ending = LANES
        widths = [w * LANES for w in split_degrees(tiles - 1)]
    else:
        ending = 0
        widths = [blocks]
    offsets = [sum(widths[:c]) for c in range(len(widths))]

    def send(value, x):
        return lax.ppermute(value, "blk", partner(x, n))

    *cuts, own = open_blocks(
        legendre,
        fourier_cycles,
        cycle_weight,
        cluster_cycles,
        cluster_flux,
        [[(across, 0, widths[0])]],
        [0],
        blocks,
    )
    then, _ = lax.optimization_barrier((legendre, cuts[0]))
    pieces = [[(x, at, w)] for at, w in zip(offsets, widths) for x in order][1:]
    if ending:
        at = blocks - ending
        pieces += [[(x, at, ending), (x ^ across, at, ending)] for x in order + [0]]
    carry = [p[0] for p in pieces].index((across, offsets[1], widths[1])) if ending else 0
    *more, home = cut(then, weights, pieces + [[(0, 0, blocks)]], blocks, carry, ending)
    cuts += more
    sent = []
    for offset in offsets:
        sent.append({x: (send(cuts.pop(0), x), 0) for x in order})
    if ending:
        last_parts = {x: send(cuts.pop(0), x) for x in order}
        (last_parts[0],) = cuts
    near = send(legendre, 1)
    for offset, parts in zip(offsets, sent):
        parts[0] = (home, offset)
        parts[1] = (near, None)

    carrier = sent[0][across][0]
    cycles = {0: (own, 0), across: (carrier, widths[0])}
    bit = n // 4
    while bit:
        for x in list(cycles):
            value, at = cycles[x]
            cycles[x ^ bit] = (send(value[:, :, at : at + columns], bit), 0)
        bit //= 2
    analysis = prepare([cycles[x] for x in range(n)])
    response, limits = response_rows(order_per_slot, weights, skies, columns)

    total = None
    for c, (offset, width) in enumerate(zip(offsets, widths)):
        final = c == len(offsets) - 1
        result = chunk(
            limits,
            [sent[c][x] for x in range(n)],
            analysis,
            weights,
            total,
            response if final else None,
            blocks,
            offset,
            width,
            2 if final and ending else 0,
        )
        total = result[0]
    returned = [send(result[x], x) for x in far + [1]]
    own = result[0]
    if ending:
        last_parts[1] = near
        own, beside = ends(
            limits,
            [sent[-1][x] for x in range(n)],
            [last_parts[x] for x in range(n)],
            analysis,
            weights,
            sent[1][across][0],
            widths[1],
            own,
            across,
            blocks,
            offsets[-1],
            widths[-1],
        )
        returned.append(send(beside, 1))
    return finish([own] + returned, fourier_cycles.shape, float(legendre.shape[2]))


def solution(mesh):
    return jax.shard_map(
        body,
        mesh=mesh,
        in_specs=(
            P("order", "blk", None),
            P("order", "blk", None),
            P("blk"),
            P("blk", None, None),
            P("order", None),
            P("order", None, None),
            P("order"),
        ),
        out_specs=P("order", "blk", None),
        check_vma=False,
    )
```
